32 devices in a mesh: frame: 16 (over z, y, core), head: 2 (over x).
Axes of the slice: x: 2, y: 2, z: 4, core: 2. Of those that a mesh axis runs over, the one named last changes fastest.
Arguments:
- tokens: bfloat16 [4096, 3072], P('frame'), may hold values from -6 to 6
- w_qkv: bfloat16 [3, 3072, 768], P(None, None, 'head'), may hold values from -0.109375 to 0.109375
- norm_gains: float32 [2, 768], P(None, 'head'), may hold values from 0.8 to 2.5
- w_out: bfloat16 [768, 3072], P('head'), may hold values from -0.3125 to 0.3125
- near_mask: int32 [32, 4], P('frame'), may hold values 0 or 1
- far_pattern: int32 [32, 32], P('frame'), may hold values from 0 to 1, as said below
- window: int32 [16], replicated, may hold values from 1 to 256, as said below
Outputs:
- layer_out: bfloat16 [4096, 3072], P('frame', 'head')
- checksum: float32 [4096], P('frame')
The draws below stay inside these ranges and needn't reach their ends.
Inputs may be any that keep to these rules, and one draw needn't show every extreme that they name: `far_pattern`: 0 or 1; entries whose two blocks lie in slabs less than two apart are never read. Entry d is the window for slabs d apart; entry 0 is 256.
All inputs are finite; a program needn't handle non-finite values. No bound on the sum of `near_mask` on one device may be relied on, other than what follows from the above.
Results may differ from the reference program's by a relative error of at most 0.015.
Values may be sent and summed in bfloat16 or wider, within the bound.
No kernel may reach another device: no remote copies, remote signals or barrier semaphores. Data moves between devices by JAX's collectives and lax.ppermute only.
A program may use at most 128 MiB of HBM per device.

```python
import math
import jax
import jax.numpy as jnp
from jax import lax

D = 3072
HD = 128
HEADS = 6
TOK_DEV = 256
BLK = 128
NBLK = 2
TOKENS = 4096
QBLOCKS = 32


def draw_far_pattern(key, part):
    density_key = jax.random.fold_in(key, 11)
    grid_key = jax.random.fold_in(key, 12)
    slab_count = QBLOCKS // NBLK
    density = jax.random.randint(density_key, (slab_count,), 1, 9)
    density_rows = jnp.repeat(density, NBLK)
    draws_grid = jax.random.randint(grid_key, (QBLOCKS, QBLOCKS), 0, 8)
    return (draws_grid < density_rows[:, None]).astype(jnp.int32)


def draw_window(key, part):
    slab_count = QBLOCKS // NBLK
    base_draw = jax.random.randint(jax.random.fold_in(key, 21), (slab_count,), TOK_DEV // 4, TOK_DEV + 1)
    distance = jnp.arange(slab_count)
    narrowed = jnp.maximum(base_draw // (1 + distance // 8), 1)
    return jnp.where(distance == 0, TOK_DEV, narrowed).astype(jnp.int32)


def with_ends(values, key, smallest, top_value):
    extent = values.shape
    spot = [jax.random.randint(jax.random.fold_in(key, axis), (), 0, extent[axis]) for axis in range(len(extent))]
    values = values.at[tuple(spot)].set(smallest)
    longest = extent.index(max(extent))
    spot[longest] = (spot[longest] + 1) % extent[longest]
    return values.at[tuple(spot)].set(top_value)


def strengthened(entries, own_key, source, target, blocks, factor):
    def block_of(dim):
        return (jnp.arange(entries.shape[dim]) // (entries.shape[dim] // blocks)).reshape((-1,) + (1,) * (entries.ndim - 1 - dim))

    near = jax.random.permutation(own_key, blocks)[block_of(target)]
    other_side = (block_of(target) + blocks // 2) % blocks
    return jnp.where((block_of(source) == near) | (block_of(source) == other_side), factor * entries, entries)


def steps_of(own_key, dims, shards, least, largest):
    level = 1.0
    for axis_at, shards_of in shards:
        heights = jax.random.uniform(jax.random.fold_in(jax.random.fold_in(own_key, 6), axis_at), (shards_of,), jnp.float32, least / len(shards), largest / len(shards))
        level = level * jnp.repeat(jnp.exp(heights), dims[axis_at] // shards_of).reshape((-1,) + (1,) * (len(dims) - 1 - axis_at))
    return level


def gaussian(key, shape, width, bound, split=(), held_as=jnp.bfloat16):
    factor_of = steps_of(key, shape, split, -0.22, 0.18) if split else 1.0
    array = jax.random.normal(key, shape, jnp.float32) * width * factor_of
    return jnp.minimum(jnp.maximum(array, -bound), bound).astype(held_as)


def heavy_noise(key, shape, deviation, bound, pieces, heavy, dtype=jnp.bfloat16):
    drawn = deviation * jax.random.normal(key, shape, jnp.float32)
    if pieces:
        drawn = drawn * steps_of(key, shape, pieces, -0.22, 0.18)
    return jnp.clip(strengthened(drawn, jax.random.fold_in(key, 3), *heavy), -bound, bound).astype(dtype)


def setup_inputs(seed: int = 0) -> dict:
    arg_keys = jax.random.split(jax.random.key(seed), 8)
    tokens = gaussian(arg_keys[0], (TOKENS, D), 1.0, 6.0, ((0, 16),))
    w_qkv = gaussian(arg_keys[1], (3, D, HEADS * HD), D ** -0.5, 0.109375, ((2, 2),))
    norm_gains = jnp.clip(jnp.exp(math.log(2.5) - 1.13943427 * jax.random.uniform(arg_keys[2], (2, HEADS * HD), jnp.float32) ** steps_of(arg_keys[2], (2, HEADS * HD), ((1, 2),), -0.2, 0.2)), 0.8, 2.5)
    w_out = heavy_noise(arg_keys[3], (HEADS * HD, D), (HEADS * HD) ** -0.5, 0.3125, ((0, 2),), (0, 1, 2, 2.0))
    near_mask = with_ends((jax.random.randint(arg_keys[4], (QBLOCKS, 2 * NBLK), 0, 4) < 3).astype(jnp.int32), jax.random.fold_in(arg_keys[4], 1), 0, 1)
    far_pattern = draw_far_pattern(jax.random.fold_in(arg_keys[7], 71), 0)
    window = draw_window(jax.random.fold_in(arg_keys[7], 71), 0)
    return dict(tokens=tokens, w_qkv=w_qkv, norm_gains=norm_gains, w_out=w_out, near_mask=near_mask, far_pattern=far_pattern, window=window)


def normed_heads(values, gain_row):
    shaped = values.reshape(values.shape[0], -1, HD)
    factor = lax.rsqrt(lax.optimization_barrier(jnp.mean(shaped * shaped, axis=-1, keepdims=True)) + 1e-06)
    return shaped * factor * gain_row.reshape(-1, HD)

def reference(tokens, w_qkv, norm_gains, w_out, near_mask, far_pattern, window):
    query = jnp.dot(tokens, w_qkv[0], preferred_element_type=jnp.float32)
    key_full = jnp.dot(tokens, w_qkv[1], preferred_element_type=jnp.float32)
    value_full = jnp.dot(tokens, w_qkv[2], preferred_element_type=jnp.float32)
    queries = lax.optimization_barrier((normed_heads(query, norm_gains[0]) * HD ** (-0.5)).astype(jnp.bfloat16))
    keys_head = lax.optimization_barrier(normed_heads(key_full, norm_gains[1]).astype(jnp.bfloat16))
    values_head = lax.optimization_barrier(value_full.astype(jnp.bfloat16).reshape(TOKENS, -1, HD))
    keys_wide = keys_head.astype(jnp.float32)
    values_wide = values_head.astype(jnp.float32)
    n_blocks = TOK_DEV // BLK
    key_index = jnp.arange(TOKENS).astype(jnp.int32)
    key_slab = key_index // TOK_DEV
    key_pos = key_index % TOK_DEV
    key_block = key_index // BLK
    position = jnp.arange(TOK_DEV).astype(jnp.int32)

    def one_slab(slab_id):
        query_rows = lax.dynamic_slice_in_dim(queries, slab_id * TOK_DEV, TOK_DEV, 0).astype(jnp.float32)
        far_rows = lax.dynamic_slice_in_dim(far_pattern, slab_id * n_blocks, n_blocks, 0)
        near_rows = lax.dynamic_slice_in_dim(near_mask, slab_id * n_blocks, n_blocks, 0)
        distance = jnp.abs(key_slab - slab_id)
        key_side = jnp.where(key_slab < slab_id, 0, 1).astype(jnp.int32)
        near_cols = (key_side * n_blocks + key_pos // BLK).astype(jnp.int32)
        far_sel = far_rows[:, key_block]
        near_sel = near_rows[:, near_cols]
        chosen = jnp.where(distance == 0, 1, jnp.where(distance == 1, near_sel, far_sel))
        chosen = jnp.repeat(chosen, BLK, axis=0)
        key_limit = window[distance]
        allowed = (chosen > 0) & (jnp.abs(position[:, None] - key_pos[None, :]) < key_limit[None, :])
        scores = jnp.einsum('qhd,khd->hqk', query_rows, keys_wide)
        weights = jnp.where(allowed[None], jnp.exp(scores), 0.0)
        total = lax.optimization_barrier(jnp.sum(weights, axis=-1))
        rounded = lax.optimization_barrier(weights.astype(jnp.bfloat16)).astype(jnp.float32)
        numer = jnp.einsum('hqk,khd->qhd', rounded, values_wide)
        return (numer / total.T[:, :, None]).reshape(TOK_DEV, -1).astype(jnp.bfloat16)
    slab_ids = jnp.arange(TOKENS // TOK_DEV).astype(jnp.int32)
    attended = lax.map(one_slab, slab_ids).reshape(TOKENS, -1)
    full = jnp.dot(attended, w_out, preferred_element_type=jnp.float32)
    checksum = lax.optimization_barrier(jnp.sum(full, axis=1)) * D ** (-0.5)
    return (full.astype(jnp.bfloat16), checksum)
```

```python
import functools

import jax
import jax.numpy as jnp
from jax import lax
from jax.experimental import pallas as pl
from jax.experimental.pallas import tpu as pltpu
from jax.sharding import PartitionSpec as P

D = 3072
HD = 128
BLK = 128
EPS = 1e-06
PAD = 16
F32 = jnp.float32
BF16 = jnp.bfloat16
VMEM = pltpu.VMEM
SMEM = pltpu.SMEM
LIMIT = 48 * 1024 * 1024


def normed(values, gains, scale):
    parts = []
    for first in range(0, values.shape[1], HD):
        head = values[:, first : first + HD]
        factor = lax.rsqrt(jnp.mean(head * head, axis=-1, keepdims=True) + EPS)
        parts.append(head * factor * gains[:, first : first + HD] * scale)
    return jnp.concatenate(parts, axis=1)


def kv_kernel(tokens, w_key, w_value, gains, out, key_sum, value_sum):
    step = pl.program_id(0)
    key_part = jnp.dot(tokens[...], w_key[0], preferred_element_type=F32)
    value_part = jnp.dot(tokens[...], w_value[0], preferred_element_type=F32)

    @pl.when(step == 0)
    def _():
        key_sum[...] = key_part
        value_sum[...] = value_part

    @pl.when(step > 0)
    def _():
        key_sum[...] += key_part
        value_sum[...] += value_part

    @pl.when(step == pl.num_programs(0) - 1)
    def _():
        rows = tokens.shape[0]
        out[:rows, :] = normed(key_sum[...], gains[1:2, :], 1.0).astype(BF16)
        out[rows:, :] = value_sum[...].astype(BF16)


def project_kv(tokens, w_qkv, gains):
    rows, width = tokens.shape
    cols = w_qkv.shape[2]
    deep = width // 4
    return pl.pallas_call(
        kv_kernel,
        grid=(width // deep,),
        in_specs=[
            pl.BlockSpec((rows, deep), lambda i: (0, i)),
            pl.BlockSpec((1, deep, cols), lambda i: (1, i, 0)),
            pl.BlockSpec((1, deep, cols), lambda i: (2, i, 0)),
            pl.BlockSpec((2, cols), lambda i: (0, 0)),
        ],
        out_specs=pl.BlockSpec((2 * rows, cols), lambda i: (0, 0)),
        out_shape=jax.ShapeDtypeStruct((2 * rows, cols), BF16),
        scratch_shapes=[VMEM((rows, cols), F32), VMEM((rows, cols), F32)],
        compiler_params=pltpu.CompilerParams(vmem_limit_bytes=LIMIT),
        cost_estimate=pl.CostEstimate(
            flops=4 * rows * width * cols,
            bytes_accessed=2 * rows * width + 4 * width * cols,
            transcendentals=rows,
        ),
        name="project_kv",
    )(tokens, w_qkv, w_qkv, gains)


def q_kernel(tokens, w_query, gains, out, query_sum):
    step = pl.program_id(0)
    part = jnp.dot(tokens[...], w_query[0], preferred_element_type=F32)

    @pl.when(step == 0)
    def _():
        query_sum[...] = part

    @pl.when(step > 0)
    def _():
        query_sum[...] += part

    @pl.when(step == pl.num_programs(0) - 1)
    def _():
        out[...] = normed(query_sum[...], gains[0:1, :], HD ** (-0.5)).astype(BF16)


def project_q(tokens, w_qkv, gains):
    rows, width = tokens.shape
    cols = w_qkv.shape[2]
    deep = width // 4
    return pl.pallas_call(
        q_kernel,
        grid=(width // deep,),
        in_specs=[
            pl.BlockSpec((rows, deep), lambda i: (0, i)),
            pl.BlockSpec((1, deep, cols), lambda i: (0, i, 0)),
            pl.BlockSpec((2, cols), lambda i: (0, 0)),
        ],
        out_specs=pl.BlockSpec((rows, cols), lambda i: (0, 0)),
        out_shape=jax.ShapeDtypeStruct((rows, cols), BF16),
        scratch_shapes=[VMEM((rows, cols), F32)],
        compiler_params=pltpu.CompilerParams(vmem_limit_bytes=LIMIT),
        cost_estimate=pl.CostEstimate(
            flops=2 * rows * width * cols,
            bytes_accessed=2 * rows * width + 2 * width * cols,
            transcendentals=rows,
        ),
        name="project_q",
    )(tokens, w_qkv, gains)


def split3(values):
    high = values.astype(BF16)
    rest = values - high.astype(F32)
    mid = rest.astype(BF16)
    low = (rest - mid.astype(F32)).astype(BF16)
    return high, mid, low


def w_kernel(n_head, place, w_out, sums, payload):
    rows, width = w_out.shape
    cols = width // n_head
    ones = jnp.ones((8, width), BF16)
    total = lax.dot_general(
        ones, w_out[...], (((1,), (1,)), ((), ())), preferred_element_type=F32
    )
    high, mid, low = split3(total)
    row = lax.broadcasted_iota(jnp.int32, (8, rows), 0)
    high, mid, low = high.astype(F32), mid.astype(F32), low.astype(F32)
    packed = jnp.where(row == 0, high, jnp.where(row == 1, mid, jnp.where(row == 2, low, 0.0)))
    packed = jnp.concatenate([packed, jnp.zeros((PAD - 8, rows), F32)], axis=0).astype(BF16)
    sums[...] = packed
    for k in range(1, n_head):
        target = lax.rem(place[0] + k, n_head)
        first = pl.multiple_of(target * cols, HD)
        payload[k - 1, :rows, :] = w_out[:, pl.ds(first, cols)]
        payload[k - 1, rows:, :] = jnp.zeros((PAD, cols), BF16)
        payload[k - 1, rows:, :rows] = packed


def prepare_w(place, w_out, n_head):
    rows, width = w_out.shape
    cols = width // n_head
    return pl.pallas_call(
        functools.partial(w_kernel, n_head),
        in_specs=[pl.BlockSpec(memory_space=SMEM), pl.BlockSpec(memory_space=VMEM)],
        out_specs=[pl.BlockSpec(memory_space=VMEM)] * 2,
        out_shape=[
            jax.ShapeDtypeStruct((PAD, rows), BF16),
            jax.ShapeDtypeStruct((n_head - 1, rows + PAD, cols), BF16),
        ],
        compiler_params=pltpu.CompilerParams(vmem_limit_bytes=LIMIT),
        cost_estimate=pl.CostEstimate(
            flops=2 * 8 * rows * width, bytes_accessed=4 * rows * width, transcendentals=0
        ),
        name="prepare_w",
    )(place, w_out)


def block_limit(masks, near_cols, window, query_slab, key_slab, query_block, key_block, n_blocks):
    distance = jnp.abs(key_slab - query_slab)
    side = jnp.where(key_slab < query_slab, 0, 1)
    near = masks[query_block, side * n_blocks + key_block]
    far = masks[query_block, near_cols + key_slab * n_blocks + key_block]
    chosen = jnp.where(distance == 0, 1, jnp.where(distance == 1, near, far))
    return jnp.where(chosen > 0, window[distance], 0)


def attend_kernel(n_chunks, first, last, near_cols, ids, own, sibling, window, queries, sib_queries, *rest):
    chunks, rest = rest[: 2 * n_chunks], rest[2 * n_chunks :]
    if not first:
        num_in, den_in, rest = rest[0], rest[1], rest[2:]
    rows, cols = queries.shape
    n_blocks = rows // BLK
    gap = jnp.abs(
        lax.broadcasted_iota(jnp.int32, (rows, rows), 0)
        - lax.broadcasted_iota(jnp.int32, (rows, rows), 1)
    )
    row_block = lax.broadcasted_iota(jnp.int32, (rows, rows), 0) // BLK
    col_block = lax.broadcasted_iota(jnp.int32, (rows, rows), 1) // BLK
    for side, (masks, q_ref) in enumerate(((own, queries), (sibling, sib_queries))):
        allowed = []
        for c in range(n_chunks):
            limit = jnp.zeros((rows, rows), jnp.int32)
            for i in range(n_blocks):
                for j in range(n_blocks):
                    here = block_limit(
                        masks, near_cols, window, ids[side], ids[2 + c], i, j, n_blocks
                    )
                    limit = jnp.where((row_block == i) & (col_block == j), here, limit)
            allowed.append(gap < limit)
        lo = side * rows
        for h in range(cols // HD):
            span = slice(h * HD, (h + 1) * HD)
            if first:
                num = jnp.zeros((rows, HD), F32)
                den = jnp.zeros((rows, HD), F32)
            else:
                num = num_in[lo : lo + rows, span]
                den = den_in[lo : lo + rows, span]
            for c in range(n_chunks):
                key_ref, value_ref = chunks[2 * c], chunks[2 * c + 1]
                scores = lax.dot_general(
                    q_ref[:, span],
                    key_ref[0, :, span],
                    (((1,), (1,)), ((), ())),
                    preferred_element_type=F32,
                )
                weights = jnp.where(allowed[c], jnp.exp(scores), 0.0)
                for b in range(0, rows, HD):
                    den = den + weights[:, b : b + HD]
                num = num + jnp.dot(
                    weights.astype(BF16), value_ref[0, :, span], preferred_element_type=F32
                )
            if not last:
                num_out, den_out = rest
                num_out[lo : lo + rows, span] = num
                den_out[lo : lo + rows, span] = den
            else:
                out = rest[side]
                out[:, span] = num
                if h == 0:
                    totals = jnp.zeros((rows, HD), F32)
                lane = lax.broadcasted_iota(jnp.int32, (rows, HD), 1)
                totals = jnp.where(lane == h, jnp.sum(den, axis=1, keepdims=True), totals)
        if last:
            rest[side][:, cols:] = totals


def attend(ids, own, sibling, window, near_cols, queries, sib_queries, chunks, totals, last):
    rows, cols = queries.shape
    first = totals is None
    smem = pl.BlockSpec(memory_space=SMEM)
    vmem = pl.BlockSpec(memory_space=VMEM)
    in_specs = [smem] * 4 + [vmem] * 2
    operands = [ids, own, sibling, window, queries, sib_queries]
    for keys, key_block, values, value_block in chunks:
        for array, block in ((keys, key_block), (values, value_block)):
            operands.append(array.reshape(-1, rows, cols))
            in_specs.append(pl.BlockSpec((1, rows, cols), lambda i, block=block: (block, 0, 0)))
    if not first:
        operands += list(totals)
        in_specs += [vmem] * 2
    if last:
        out_shape = [jax.ShapeDtypeStruct((rows, cols + HD), F32)] * 2
    else:
        out_shape = [jax.ShapeDtypeStruct((2 * rows, cols), F32)] * 2
    work = 2 * rows * rows * len(chunks)
    return pl.pallas_call(
        functools.partial(attend_kernel, len(chunks), first, last, near_cols),
        grid=(1,),
        in_specs=in_specs,
        out_specs=[vmem] * 2,
        out_shape=out_shape,
        compiler_params=pltpu.CompilerParams(vmem_limit_bytes=LIMIT),
        cost_estimate=pl.CostEstimate(
            flops=4 * work * cols,
            bytes_accessed=4 * rows * cols * (len(chunks) + 4),
            transcendentals=work * cols // HD,
        ),
        name="attend",
    )(*operands)


def finish_kernel(kept, got, out):
    cols = out.shape[1]
    totals = kept[:, cols:] + got[:, cols:]
    for h in range(cols // HD):
        span = slice(h * HD, (h + 1) * HD)
        out[:, span] = ((kept[:, span] + got[:, span]) / totals[:, h : h + 1]).astype(BF16)


def finish(kept, got):
    rows, wide = kept.shape
    return pl.pallas_call(
        finish_kernel,
        in_specs=[pl.BlockSpec(memory_space=VMEM)] * 2,
        out_specs=pl.BlockSpec(memory_space=VMEM),
        out_shape=jax.ShapeDtypeStruct((rows, wide - HD), BF16),
        compiler_params=pltpu.CompilerParams(vmem_limit_bytes=LIMIT),
        name="finish",
    )(kept, got)


def out_kernel(n_head, place, *refs):
    attended, weights = refs[:n_head], refs[n_head : 2 * n_head]
    sums = refs[2 * n_head : 3 * n_head]
    out, checksum, parts = refs[3 * n_head :]
    total = jnp.dot(attended[0][...], weights[0][...], preferred_element_type=F32)
    for k in range(1, n_head):
        total = total + jnp.dot(attended[k][...], weights[k][0], preferred_element_type=F32)
    out[...] = total.astype(BF16)

    @pl.when(pl.program_id(0) == 0)
    def _():
        for k in range(n_head):
            rows = attended[k].shape[1]
            summed = sums[k][...] if k == 0 else sums[k][0, :, :rows]
            dots = lax.dot_general(
                summed, attended[k][...], (((1,), (1,)), ((), ())), preferred_element_type=F32
            )
            owner = lax.rem(place[0] - k + n_head, n_head)
            parts[pl.ds(owner, 1), :] = dots[0:1, :] + (dots[1:2, :] + dots[2:3, :])
        sum_all = parts[0:1, :]
        for k in range(1, n_head):
            sum_all = sum_all + parts[k : k + 1, :]
        checksum[...] = sum_all * D ** (-0.5)


def project_out(place, attended, w_out, sums, received):
    n_head = len(attended)
    rows, depth = attended[0].shape
    cols = w_out.shape[1] // n_head
    tile = cols // 3
    tiles = cols // tile
    grid_spec = pltpu.PrefetchScalarGridSpec(
        num_scalar_prefetch=1,
        grid=(tiles,),
        in_specs=[pl.BlockSpec((rows, depth), lambda i, place: (0, 0))] * n_head
        + [pl.BlockSpec((depth, tile), lambda i, place: (0, place[0] * tiles + i))]
        + [pl.BlockSpec((1, depth, tile), lambda i, place: (0, 0, i))] * (n_head - 1)
        + [pl.BlockSpec((PAD, depth), lambda i, place: (0, 0))]
        + [pl.BlockSpec((1, PAD, cols), lambda i, place: (0, depth // PAD, 0))] * (n_head - 1),
        out_specs=[
            pl.BlockSpec((rows, tile), lambda i, place: (0, i)),
            pl.BlockSpec((1, rows), lambda i, place: (0, 0)),
        ],
        scratch_shapes=[VMEM((max(n_head, 8), rows), F32)],
    )
    layer_out, checksum = pl.pallas_call(
        functools.partial(out_kernel, n_head),
        grid_spec=grid_spec,
        out_shape=[
            jax.ShapeDtypeStruct((rows, cols), BF16),
            jax.ShapeDtypeStruct((1, rows), F32),
        ],
        compiler_params=pltpu.CompilerParams(vmem_limit_bytes=LIMIT),
        name="project_out",
    )(place, *attended, w_out, *received, sums, *received)
    return layer_out, checksum.reshape(rows)


def per_device(tokens, w_qkv, norm_gains, w_out, near_mask, far_pattern, window):
    rows = tokens.shape[0]
    frame = lax.axis_index("frame")
    place = lax.axis_index("head").astype(jnp.int32).reshape(1)
    n_frame = lax.axis_size("frame")
    n_head = lax.axis_size("head")
    chips = n_frame // 2
    half = chips // 2
    order = [2 * p if p < half else 2 * (chips - 1 - p) + 1 for p in range(chips)]

    def ring(by):
        return [
            (order[p] * 2 + core, order[(p + by) % chips] * 2 + core)
            for p in range(chips)
            for core in range(2)
        ]

    onward, backward = ring(1), ring(-1)
    siblings = [(i, i ^ 1) for i in range(n_frame)]
    chip, core = frame // 2, frame % 2
    spot = jnp.where(chip % 2 == 0, chip // 2, chips - 1 - chip // 2)

    def slab_at(offset):
        at = (spot + offset + chips) % chips
        return 2 * jnp.where(at < half, 2 * at, 2 * (chips - 1 - at) + 1) + core

    def ids(*offsets):
        values = [frame, frame + 1 - 2 * core] + [slab_at(o) for o in offsets]
        return jnp.stack([v.astype(jnp.int32) for v in values])

    kv = project_kv(tokens, w_qkv, norm_gains)
    up, down = kv, kv
    arrivals = []
    steps = (chips - 1) // 2
    for s in range(1, steps + 1):
        up = lax.ppermute(up, "frame", onward)
        down = lax.ppermute(down, "frame", backward)
        arrivals.append((up, down))
    last_keys = lax.ppermute(up[:rows], "frame", onward)
    last_values = lax.ppermute(down[rows:], "frame", backward)

    queries = project_q(tokens, w_qkv, norm_gains)
    sib_queries = lax.ppermute(queries, "frame", siblings)
    masks = jnp.concatenate([near_mask, far_pattern], axis=1)
    sib_masks = lax.ppermute(masks, "frame", siblings)
    sums, payload = prepare_w(place, w_out, n_head)
    received = [
        lax.ppermute(
            payload[k - 1 : k], "head", [(i, (i + k) % n_head) for i in range(n_head)]
        )
        for k in range(1, n_head)
    ]

    near_cols = near_mask.shape[1]
    common = (masks, sib_masks, window, near_cols, queries, sib_queries)
    totals = attend(ids(0), *common, [(kv, 0, kv, 1)], None, False)
    for s, (up, down) in enumerate(arrivals, 1):
        totals = attend(ids(-s, s), *common, [(up, 0, up, 1), (down, 0, down, 1)], totals, False)
    kept, sent = attend(ids(-half), *common, [(last_keys, 0, last_values, 0)], totals, True)
    got = lax.ppermute(sent, "frame", siblings)
    own = finish(kept, got)
    attended = [own] + [
        lax.ppermute(own, "head", [(i, (i + k) % n_head) for i in range(n_head)])
        for k in range(1, n_head)
    ]
    return project_out(place, attended, w_out, sums, received)


def solution(mesh):
    in_specs = (
        P("frame", None),
        P(None, None, "head"),
        P(None, "head"),
        P("head", None),
        P("frame", None),
        P("frame", None),
        P(),
    )
    out_specs = (P("frame", "head"), P("frame"))
    return jax.shard_map(
        per_device, mesh=mesh, in_specs=in_specs, out_specs=out_specs, check_vma=False
    )
```

```python
import functools

import jax
import jax.numpy as jnp
from jax import lax
from jax.experimental import pallas as pl
from jax.experimental.pallas import tpu as pltpu
from jax.sharding import PartitionSpec as P

D = 3072
HD = 128
BLK = 128
EPS = 1e-06
PAD = 16
BARRED = -1e30
F32 = jnp.float32
BF16 = jnp.bfloat16
VMEM = pltpu.VMEM
SMEM = pltpu.SMEM
MIB = 1024 * 1024
IN_VMEM = pl.BlockSpec(memory_space=VMEM)
IN_SMEM = pl.BlockSpec(memory_space=SMEM)
IN_HBM = pl.BlockSpec(memory_space=pltpu.HBM)
ANYWHERE = pl.BlockSpec(memory_space=pl.ANY)


def params(mib):
    return pltpu.CompilerParams(vmem_limit_bytes=mib * MIB)


def cost(microseconds):
    return pl.CostEstimate(
        flops=int(microseconds * 0), bytes_accessed=int(microseconds * 0), transcendentals=0
    )


def normed(values, gains, scale):
    parts = []
    for first in range(0, values.shape[1], HD):
        head = values[:, first : first + HD]
        factor = lax.rsqrt(jnp.mean(head * head, axis=-1, keepdims=True) + EPS)
        parts.append(head * factor * gains[:, first : first + HD] * scale)
    return jnp.concatenate(parts, axis=1)


def project_kernel(steps, tokens, w_qkv, gains, near_mask, far_pattern, kv, queries, *scratch):
    token_buf, w_buf, gain_buf, near_buf, far_buf, total, sems, small_sems = scratch
    rows, width = tokens.shape
    count, _, cols = w_qkv.shape
    deep = width // steps
    copies = []
    for s in range(steps):
        span = pl.ds(s * deep, deep)
        group = [pltpu.make_async_copy(tokens.at[:, span], token_buf.at[:, span], sems.at[0, s])]
        for j in range(count):
            group.append(
                pltpu.make_async_copy(
                    w_qkv.at[j, span], w_buf.at[span, pl.ds(j * cols, cols)], sems.at[1 + j, s]
                )
            )
        for copy in group:
            copy.start()
        copies.append(group)
    small = [
        pltpu.make_async_copy(source, target, small_sems.at[i])
        for i, (source, target) in enumerate(
            ((gains, gain_buf), (near_mask, near_buf), (far_pattern, far_buf))
        )
    ]
    for copy in small:
        copy.start()
    for s in range(steps):
        for copy in copies[s]:
            copy.wait()
        span = slice(s * deep, (s + 1) * deep)
        part = jnp.dot(token_buf[:, span], w_buf[span, :], preferred_element_type=F32)
        if s == 0:
            total[...] = part
        elif s < steps - 1:
            total[...] += part
    part = total[...] + part
    for copy in small:
        copy.wait()
    query, key, value = (part[:, j * cols : (j + 1) * cols] for j in range(count))
    kv[:rows, :] = normed(key, gain_buf[1:2, :], 1.0).astype(BF16)
    kv[rows:, :] = value.astype(BF16)
    queries[:rows, :] = normed(query, gain_buf[0:1, :], HD ** (-0.5)).astype(BF16)
    n_blocks, n_near = near_mask.shape
    queries[rows:, :] = jnp.zeros((PAD, cols), BF16)
    queries[rows : rows + n_blocks, :n_near] = near_buf[...].astype(F32).astype(BF16)
    queries[rows : rows + n_blocks, HD : HD + far_pattern.shape[1]] = (
        far_buf[...].astype(F32).astype(BF16)
    )


def project(tokens, w_qkv, gains, near_mask, far_pattern):
    rows, width = tokens.shape
    count, _, cols = w_qkv.shape
    steps = 4
    return pl.pallas_call(
        functools.partial(project_kernel, steps),
        in_specs=[ANYWHERE] * 5,
        out_specs=[IN_VMEM] * 2,
        out_shape=[
            jax.ShapeDtypeStruct((2 * rows, cols), BF16),
            jax.ShapeDtypeStruct((rows + PAD, cols), BF16),
        ],
        scratch_shapes=[
            VMEM((rows, width), BF16),
            VMEM((width, count * cols), BF16),
            VMEM(gains.shape, F32),
            VMEM(near_mask.shape, jnp.int32),
            VMEM(far_pattern.shape, jnp.int32),
            VMEM((rows, count * cols), F32),
            pltpu.SemaphoreType.DMA((1 + count, steps)),
            pltpu.SemaphoreType.DMA((3,)),
        ],
        compiler_params=params(56),
        cost_estimate=cost(5.0),
        name="project",
    )(tokens, w_qkv, gains, near_mask, far_pattern)


def split_sum(values):
    high = values.astype(BF16).astype(F32)
    mid = (values - high).astype(BF16).astype(F32)
    return high, mid, values - high - mid


def w_kernel(n_head, place, w_out, _, sums, payload):
    rows, width = w_out.shape
    cols = width // n_head
    total = lax.dot_general(
        jnp.ones((8, width), BF16), w_out[...], (((1,), (1,)), ((), ())), preferred_element_type=F32
    )
    high, mid, low = split_sum(total)
    row = lax.broadcasted_iota(jnp.int32, (8, rows), 0)
    packed = jnp.where(row == 0, high, jnp.where(row == 1, mid, jnp.where(row == 2, low, 0.0)))
    packed = jnp.concatenate([packed, jnp.zeros((PAD - 8, rows), F32)], axis=0).astype(BF16)
    sums[...] = packed
    share = payload.shape[1]
    for k in range(1, n_head):
        target = lax.rem(place[0] + k, n_head)
        first = pl.multiple_of(target * cols, HD)

        @pl.when(place[1] == 0)
        def _():
            payload[k - 1] = w_out[:share, pl.ds(first, cols)]

        @pl.when(place[1] == 1)
        def _():
            payload[k - 1, : rows - share, :] = w_out[share:, pl.ds(first, cols)]
            payload[k - 1, rows - share :, :] = jnp.zeros((2 * share - rows, cols), BF16)
            payload[k - 1, rows - share : rows - share + PAD, :rows] = packed


def prepare_w(place, w_out, n_head, before):
    rows, width = w_out.shape
    cols = width // n_head
    share = (rows + 2 * PAD) // 2
    return pl.pallas_call(
        functools.partial(w_kernel, n_head),
        in_specs=[IN_SMEM, IN_VMEM, IN_VMEM],
        out_specs=[IN_VMEM] * 2,
        out_shape=[
            jax.ShapeDtypeStruct((PAD, rows), BF16),
            jax.ShapeDtypeStruct((n_head - 1, share, cols), BF16),
        ],
        compiler_params=params(16),
        cost_estimate=cost(1.2),
        name="prepare_w",
    )(place, w_out, before)


def merge_kernel(place, mine, sibling, out):
    share = mine.shape[1]

    @pl.when(place[1] == 0)
    def _():
        out[:, :share, :] = mine[...]
        out[:, share:, :] = sibling[...]

    @pl.when(place[1] == 1)
    def _():
        out[:, :share, :] = sibling[...]
        out[:, share:, :] = mine[...]


def merge_w(place, mine, sibling):
    n, share, cols = mine.shape
    return pl.pallas_call(
        merge_kernel,
        in_specs=[IN_SMEM, IN_VMEM, IN_VMEM],
        out_specs=IN_VMEM,
        out_shape=jax.ShapeDtypeStruct((n, 2 * share, cols), BF16),
        compiler_params=params(16),
        cost_estimate=cost(0.4),
        name="merge_w",
    )(place, mine, sibling)


def bias_kernel(side, n_slabs, n_blocks, ids, window, queries, _, out):
    rows = n_blocks * BLK
    shifted = lax.broadcasted_iota(jnp.int32, (BLK, BLK), 0) - lax.broadcasted_iota(
        jnp.int32, (BLK, BLK), 1
    )
    gaps = {
        by: jnp.abs(shifted + by * BLK).astype(F32) for by in range(1 - n_blocks, n_blocks)
    }
    lane = lax.broadcasted_iota(jnp.int32, (PAD, queries.shape[1]), 1)
    masks = queries[rows : rows + PAD, :].astype(F32)
    query_slab = ids[side]
    for c in range(n_slabs):
        key_slab = ids[2 + c]
        distance = jnp.abs(key_slab - query_slab)
        before = jnp.where(key_slab < query_slab, 0, 1)
        first = jnp.where(distance == 1, before * n_blocks, HD + key_slab * n_blocks)
        whole = jnp.where(distance == 0, 1.0, 0.0)
        reach = window[distance].astype(F32)
        for j in range(n_blocks):
            picked = jnp.sum(jnp.where(lane == first + j, masks, 0.0), axis=1, keepdims=True)
            limit = jnp.where(jnp.maximum(picked, whole) > 0.5, reach, 0.0)
            for i in range(n_blocks):
                here = jnp.broadcast_to(limit[i : i + 1, :], (BLK, BLK))
                out[c, i * BLK : (i + 1) * BLK, j * BLK : (j + 1) * BLK] = jnp.where(
                    gaps[i - j] < here, 0.0, BARRED
                )


def biases(side, ids, window, queries, n_blocks, before):
    n_slabs = ids.shape[0] - 2
    rows = n_blocks * BLK
    return pl.pallas_call(
        functools.partial(bias_kernel, side, n_slabs, n_blocks),
        in_specs=[IN_SMEM] * 2 + [IN_VMEM] * 2,
        out_specs=IN_VMEM,
        out_shape=jax.ShapeDtypeStruct((n_slabs, rows, rows), F32),
        compiler_params=params(16),
        cost_estimate=cost(0.5),
        name="biases",
    )(ids, window, queries, before)


def attend_kernel(slabs, lone, has_totals, packed, heads, bias, queries, _, *refs):
    rows = bias.shape[1]
    chunks, refs = [], list(refs)
    for apart in lone:
        if apart:
            chunks.append((refs.pop(0), refs.pop(0)))
        else:
            both = refs.pop(0)
            chunks.append((both.at[:rows], both.at[rows:]))
    before, out = (refs[0], refs[1]) if has_totals else (None, refs[0])
    ones = jnp.ones((rows, HD), BF16)
    if packed:
        out[rows:, :] = jnp.zeros((PAD, out.shape[1]), BF16)
    for h in range(*heads):
        span = slice(h * HD, (h + 1) * HD)
        keys = jnp.concatenate([key[:, span] for key, _ in chunks], axis=0)
        scores = lax.dot_general(
            queries[:rows, span], keys, (((1,), (1,)), ((), ())), preferred_element_type=F32
        )
        weights = [
            jnp.exp(scores[:, n * rows : (n + 1) * rows] + bias[slab]).astype(BF16)
            for n, slab in enumerate(slabs)
        ]
        values = jnp.concatenate(
            [jnp.concatenate([value[:, span], ones], axis=1) for _, value in chunks], axis=0
        )
        sums = jnp.dot(jnp.concatenate(weights, axis=1), values, preferred_element_type=F32)
        if has_totals:
            sums = sums + before[h]
        if not packed:
            out[h] = sums
            continue
        span = slice((h - heads[0]) * HD, (h - heads[0] + 1) * HD)
        out[:rows, span] = sums[:, :HD].astype(BF16)
        for b in range(rows // HD):
            row = sums[b * HD : (b + 1) * HD, HD:].T[0:1, :]
            high = row.astype(BF16)
            out[rows + 2 * b : rows + 2 * b + 1, span] = high
            out[rows + 2 * b + 1 : rows + 2 * b + 2, span] = (row - high.astype(F32)).astype(BF16)


def attend(bias, queries, before, parts, totals, heads, packed, name):
    rows = bias.shape[1]
    operands = [bias, queries, before] + [array for chunk, _ in parts for array in chunk]
    if totals is not None:
        operands.append(totals)
    count = heads[1] - heads[0]
    if packed:
        shape = jax.ShapeDtypeStruct((rows + PAD, count * HD), BF16)
    else:
        shape = jax.ShapeDtypeStruct((count, rows, 2 * HD), F32)
    slabs = [slab for _, slab in parts]
    return pl.pallas_call(
        functools.partial(
            attend_kernel, slabs, [len(c) > 1 for c, _ in parts], totals is not None, packed, heads
        ),
        in_specs=[IN_VMEM] * len(operands),
        out_specs=IN_VMEM,
        out_shape=shape,
        compiler_params=params(24),
        cost_estimate=cost(0.08 * len(parts) * count + 0.15),
        name=name,
    )(*operands)


def finish_kernel(heads, kept, got, _, out):
    rows = kept.shape[1]
    for h in range(*heads):
        span = slice((h - heads[0]) * HD, (h - heads[0] + 1) * HD)
        for b in range(rows // HD):
            here = slice(b * HD, (b + 1) * HD)
            pair = got[rows : rows + PAD, span].astype(F32)
            row = pair[2 * b : 2 * b + 1, :] + pair[2 * b + 1 : 2 * b + 2, :]
            other = jnp.broadcast_to(row, (HD, HD)).T
            num = kept[h, here, :HD] + got[here, span].astype(F32)
            out[here, span] = (num / (kept[h, here, HD:] + other)).astype(BF16)


def finish(kept, got, heads, before):
    rows = kept.shape[1]
    return pl.pallas_call(
        functools.partial(finish_kernel, heads),
        in_specs=[IN_VMEM] * 3,
        out_specs=IN_VMEM,
        out_shape=jax.ShapeDtypeStruct((rows, (heads[1] - heads[0]) * HD), BF16),
        compiler_params=params(16),
        cost_estimate=cost(0.15),
        name="finish",
    )(kept, got, before)


def gate_kernel(array, _, out):
    pass


def gate(array, before):
    return pl.pallas_call(
        gate_kernel,
        in_specs=[IN_VMEM] * 2,
        out_specs=IN_VMEM,
        out_shape=jax.ShapeDtypeStruct(array.shape, array.dtype),
        input_output_aliases={0: 0},
        compiler_params=params(16),
        cost_estimate=cost(0.1),
        name="gate",
    )(array, before)


def row_dot(summed, values):
    dots = lax.dot_general(
        summed, values, (((1,), (1,)), ((), ())), preferred_element_type=F32
    )
    return dots[0:1, :] + (dots[1:2, :] + dots[2:3, :])


def early_kernel(n_head, place, own, w_out, sums, partial, parts, owners):
    cols = partial.shape[1]
    first = pl.multiple_of(place[0] * cols, HD)
    partial[...] = jnp.dot(own[...], w_out[:, pl.ds(first, cols)], preferred_element_type=F32)
    parts[...] = jnp.zeros(parts.shape, F32)
    parts[pl.ds(place[0], 1), :] = row_dot(sums[...], own[...])
    row = lax.broadcasted_iota(jnp.int32, parts.shape, 0)
    for k in range(1, n_head):
        owner = lax.rem(place[0] - k + n_head, n_head)
        owners[k - 1] = jnp.where(row == owner, 1.0, 0.0)


def project_early(place, own, w_out, sums, n_head):
    rows = own.shape[0]
    cols = w_out.shape[1] // n_head
    places = -(-n_head // 8) * 8
    return pl.pallas_call(
        functools.partial(early_kernel, n_head),
        in_specs=[IN_SMEM] + [IN_VMEM] * 3,
        out_specs=[IN_VMEM] * 3,
        out_shape=[
            jax.ShapeDtypeStruct((rows, cols), F32),
            jax.ShapeDtypeStruct((places, rows), F32),
            jax.ShapeDtypeStruct((n_head - 1, places, rows), F32),
        ],
        compiler_params=params(24),
        cost_estimate=cost(1.4),
        name="project_early",
    )(place, own, w_out, sums)


def last_kernel(n_head, depth, *refs):
    late, refs = refs[: n_head - 1], refs[n_head - 1 :]
    received, partial, parts, owners, layer_out, checksum, staged, sems = refs
    rows, cols = partial.shape
    tiles = sems.shape[0]
    tile = cols // tiles
    stores = []
    for t in range(tiles):
        here = slice(t * tile, (t + 1) * tile)
        total = partial[:, here]
        for k in range(1, n_head):
            total = total + jnp.dot(
                late[k - 1][...], received[k - 1, :depth, here], preferred_element_type=F32
            )
        staged[:, here] = total.astype(BF16)
        there = pl.ds(t * tile, tile)
        store = pltpu.make_async_copy(staged.at[:, there], layer_out.at[:, there], sems.at[t])
        store.start()
        stores.append(store)
    every = parts[...]
    for k in range(1, n_head):
        dot = row_dot(received[k - 1, depth : depth + PAD, :depth], late[k - 1][...])
        every = every + owners[k - 1] * dot
    sum_all = every[0:1, :]
    for k in range(1, n_head):
        sum_all = sum_all + every[k : k + 1, :]
    checksum[...] = sum_all * D ** (-0.5)
    for store in stores:
        store.wait()


def project_last(late, received, partial, parts, owners):
    n_head = len(late) + 1
    depth = late[0].shape[1]
    rows, cols = partial.shape
    tiles = next(t for t in (3, 2, 1) if cols % (t * HD) == 0)
    operands = [*late, received, partial, parts, owners]
    layer_out, checksum = pl.pallas_call(
        functools.partial(last_kernel, n_head, depth),
        in_specs=[IN_VMEM] * len(operands),
        out_specs=[ANYWHERE, IN_VMEM],
        out_shape=[
            jax.ShapeDtypeStruct((rows, cols), BF16),
            jax.ShapeDtypeStruct((1, rows), F32),
        ],
        scratch_shapes=[VMEM((rows, cols), BF16), pltpu.SemaphoreType.DMA((tiles,))],
        compiler_params=params(24),
        name="project_last",
    )(*operands)
    return layer_out, checksum.reshape(rows)


def per_device(tokens, w_qkv, norm_gains, w_out, near_mask, far_pattern, window):
    rows = tokens.shape[0]
    heads = w_qkv.shape[2] // HD
    n_blocks = rows // BLK
    frame = lax.axis_index("frame").astype(jnp.int32)
    place = jnp.stack([lax.axis_index("head").astype(jnp.int32), frame % 2])
    n_frame = lax.axis_size("frame")
    n_head = lax.axis_size("head")
    half = n_frame // 2
    every = (0, heads)

    def swapped(array, by):
        return lax.ppermute(array, "frame", [(i, i ^ by) for i in range(n_frame)])

    def from_head(array, k):
        return lax.ppermute(array, "head", [(i, (i + k) % n_head) for i in range(n_head)])

    spans = []
    by = half // 2
    while by > 1:
        spans.append(by)
        by //= 2
    far = sorted((o for o in range(2, half, 2) if o not in spans), key=lambda o: bin(o).count("1"))
    straight = [0] + spans + far
    slabs = straight + [o ^ 1 for o in straight]

    kv, queries = project(tokens, w_qkv, norm_gains, near_mask, far_pattern)
    other_queries = swapped(queries, half)
    chunks = {0: (kv,)}
    near = {by: swapped(kv, by) for by in spans}
    chunks[1] = (swapped(kv, 1),)
    ids = jnp.stack([frame, frame ^ half] + [frame ^ s for s in slabs])

    def some(offsets):
        return [(chunks[o], slabs.index(o)) for o in offsets]

    bias = biases(0, ids, window, queries, n_blocks, queries)
    own = attend(bias, queries, bias, some([0, 1]), None, every, False, "attend_first")
    sums, payload = prepare_w(place, w_out, n_head, own)
    mine = [from_head(payload[k - 1 : k], k) for k in range(1, n_head)]
    mine = mine[0] if len(mine) == 1 else jnp.concatenate(mine)

    low = spans[-1]
    near[low] = gate(near[low], own)
    other_bias = biases(1, ids, window, other_queries, n_blocks, near[low])
    for by in spans[:-1]:
        near[by] = gate(near[by], other_bias)
    for by in spans:
        chunks[by] = (near[by],)
        chunks[by ^ 1] = (swapped(near[by], 1),)
    keys = {by: near[by][:rows] for by in spans}
    values = {by: near[by][rows:] for by in spans}
    for o in far:
        bits = [by for by in spans if o & by]
        values[o] = swapped(values[o ^ bits[0]], bits[0])
        keys[o] = swapped(keys[o ^ bits[-1]], bits[-1])
    other = attend(
        other_bias, other_queries, own, some([0, 1] + spans), None, every, False, "other_first"
    )
    for o in far:
        keys[o], values[o] = gate(keys[o], other), gate(values[o], other)
        chunks[o] = (keys[o], values[o])
        chunks[o ^ 1] = (swapped(keys[o], 1), swapped(values[o], 1))
    middle = [by ^ 1 for by in spans] + far
    other = attend(other_bias, other_queries, other, some(middle), other, every, False, "other_middle")
    late = [o ^ 1 for o in far]
    sent = attend(other_bias, other_queries, other, some(late), other, every, True, "other_last")
    rest = spans + middle + late
    own = attend(bias, queries, sent, some(rest), own, every, False, "attend_rest")
    done = finish(own, swapped(sent, half), every, own)
    late = [from_head(done, k) for k in range(1, n_head)]
    mine = gate(mine, done)
    received = merge_w(place, mine, swapped(mine, 1))
    partial, sum_parts, owners = project_early(place, done, w_out, sums, n_head)
    return project_last(late, received, partial, sum_parts, owners)


def solution(mesh):
    in_specs = (
        P("frame", None),
        P(None, None, "head"),
        P(None, "head"),
        P("head", None),
        P("frame", None),
        P("frame", None),
        P(),
    )
    out_specs = (P("frame", "head"), P("frame"))
    return jax.shard_map(
        per_device, mesh=mesh, in_specs=in_specs, out_specs=out_specs, check_vma=False
    )
```

```python
import functools

import jax
import jax.numpy as jnp
from jax import lax
from jax.experimental import pallas as pl
from jax.experimental.pallas import tpu as pltpu
from jax.sharding import PartitionSpec as P

D = 3072
HD = 128
BLK = 128
EPS = 1e-06
PAD = 16
BARRED = -1e30
F32 = jnp.float32
BF16 = jnp.bfloat16
VMEM = pltpu.VMEM
SMEM = pltpu.SMEM
MIB = 1024 * 1024
IN_VMEM = pl.BlockSpec(memory_space=VMEM)
IN_SMEM = pl.BlockSpec(memory_space=SMEM)
IN_HBM = pl.BlockSpec(memory_space=pltpu.HBM)
ANYWHERE = pl.BlockSpec(memory_space=pl.ANY)


def params(mib):
    return pltpu.CompilerParams(vmem_limit_bytes=mib * MIB)


def cost(microseconds):
    return pl.CostEstimate(
        flops=int(microseconds * 0), bytes_accessed=int(microseconds * 0), transcendentals=0
    )


def normed(values, gains, scale):
    parts = []
    for first in range(0, values.shape[1], HD):
        head = values[:, first : first + HD]
        factor = lax.rsqrt(jnp.mean(head * head, axis=-1, keepdims=True) + EPS)
        parts.append(head * factor * gains[:, first : first + HD] * scale)
    return jnp.concatenate(parts, axis=1)


def project_kernel(steps, n_head, tokens, w_qkv, gains, near_mask, far_pattern, w_out, *refs):
    kv, queries, payload = refs[:3]
    token_buf, w_buf, gain_buf, near_buf, far_buf, total, out_buf, sems, small_sems, out_sems = refs[3:]
    rows, width = tokens.shape
    count, _, cols = w_qkv.shape
    deep = width // steps
    copies = []
    for s in range(steps):
        span = pl.ds(s * deep, deep)
        group = [pltpu.make_async_copy(tokens.at[:, span], token_buf.at[:, span], sems.at[0, s])]
        for j in range(count):
            group.append(
                pltpu.make_async_copy(
                    w_qkv.at[j, span], w_buf.at[span, pl.ds(j * cols, cols)], sems.at[1 + j, s]
                )
            )
        for copy in group:
            copy.start()
        copies.append(group)
    small = [
        pltpu.make_async_copy(source, target, small_sems.at[i])
        for i, (source, target) in enumerate(
            ((gains, gain_buf), (near_mask, near_buf), (far_pattern, far_buf))
        )
    ]
    for copy in small:
        copy.start()
    out_cols = payload.shape[2]
    place = lax.axis_index("head")
    columns = []
    for k in range(1, n_head):
        first = pl.multiple_of(lax.rem(place + k, n_head) * out_cols, HD)
        columns.append(
            (
                pltpu.make_async_copy(
                    w_out.at[:, pl.ds(first, out_cols)], out_buf.at[k - 1], out_sems.at[0, k - 1]
                ),
                pltpu.make_async_copy(out_buf.at[k - 1], payload.at[k - 1], out_sems.at[1, k - 1]),
            )
        )
    for load, _ in columns:
        load.start()
    for s in range(steps):
        for copy in copies[s]:
            copy.wait()
        span = slice(s * deep, (s + 1) * deep)
        part = jnp.dot(token_buf[:, span], w_buf[span, :], preferred_element_type=F32)
        if s == 0:
            total[...] = part
        elif s < steps - 1:
            total[...] += part
    part = total[...] + part
    for load, store in columns:
        load.wait()
        store.start()
    for copy in small:
        copy.wait()
    query, key, value = (part[:, j * cols : (j + 1) * cols] for j in range(count))
    kv[:rows, :] = normed(key, gain_buf[1:2, :], 1.0).astype(BF16)
    kv[rows:, :] = value.astype(BF16)
    queries[:rows, :] = normed(query, gain_buf[0:1, :], HD ** (-0.5)).astype(BF16)
    n_blocks, n_near = near_mask.shape
    queries[rows:, :] = jnp.zeros((PAD, cols), BF16)
    queries[rows : rows + n_blocks, :n_near] = near_buf[...].astype(F32).astype(BF16)
    queries[rows : rows + n_blocks, HD : HD + far_pattern.shape[1]] = (
        far_buf[...].astype(F32).astype(BF16)
    )
    for _, store in columns:
        store.wait()


def project(tokens, w_qkv, gains, near_mask, far_pattern, w_out, n_head):
    rows, width = tokens.shape
    count, _, cols = w_qkv.shape
    steps = 4
    return pl.pallas_call(
        functools.partial(project_kernel, steps, n_head),
        in_specs=[ANYWHERE] * 6,
        out_specs=[IN_VMEM] * 2 + [ANYWHERE],
        out_shape=[
            jax.ShapeDtypeStruct((2 * rows, cols), BF16),
            jax.ShapeDtypeStruct((rows + PAD, cols), BF16),
            jax.ShapeDtypeStruct((n_head - 1, w_out.shape[0], w_out.shape[1] // n_head), BF16),
        ],
        scratch_shapes=[
            VMEM((rows, width), BF16),
            VMEM((width, count * cols), BF16),
            VMEM(gains.shape, F32),
            VMEM(near_mask.shape, jnp.int32),
            VMEM(far_pattern.shape, jnp.int32),
            VMEM((rows, count * cols), F32),
            VMEM((n_head - 1, w_out.shape[0], w_out.shape[1] // n_head), BF16),
            pltpu.SemaphoreType.DMA((1 + count, steps)),
            pltpu.SemaphoreType.DMA((3,)),
            pltpu.SemaphoreType.DMA((2, n_head - 1)),
        ],
        compiler_params=params(56),
        cost_estimate=cost(5.0),
        name="project",
    )(tokens, w_qkv, gains, near_mask, far_pattern, w_out)


def split_sum(values):
    high = values.astype(BF16).astype(F32)
    mid = (values - high).astype(BF16).astype(F32)
    return high, mid, values - high - mid


def sums_kernel(w_out, _, sums):
    rows, width = w_out.shape
    total = lax.dot_general(
        jnp.ones((8, width), BF16), w_out[...], (((1,), (1,)), ((), ())), preferred_element_type=F32
    )
    high, mid, low = split_sum(total)
    row = lax.broadcasted_iota(jnp.int32, (8, rows), 0)
    packed = jnp.where(row == 0, high, jnp.where(row == 1, mid, jnp.where(row == 2, low, 0.0)))
    sums[...] = jnp.concatenate([packed, jnp.zeros((PAD - 8, rows), F32)], axis=0).astype(BF16)


def row_sums(w_out, before):
    return pl.pallas_call(
        sums_kernel,
        in_specs=[IN_VMEM] * 2,
        out_specs=IN_VMEM,
        out_shape=jax.ShapeDtypeStruct((PAD, w_out.shape[0]), BF16),
        compiler_params=params(16),
        cost_estimate=cost(0.8),
        name="row_sums",
    )(w_out, before)


def bias_kernel(side, n_slabs, n_blocks, ids, window, queries, _, out):
    rows = n_blocks * BLK
    shifted = lax.broadcasted_iota(jnp.int32, (BLK, BLK), 0) - lax.broadcasted_iota(
        jnp.int32, (BLK, BLK), 1
    )
    gaps = {
        by: jnp.abs(shifted + by * BLK).astype(F32) for by in range(1 - n_blocks, n_blocks)
    }
    lane = lax.broadcasted_iota(jnp.int32, (PAD, queries.shape[1]), 1)
    masks = queries[rows : rows + PAD, :].astype(F32)
    query_slab = ids[side]
    for c in range(n_slabs):
        key_slab = ids[4 + c]
        distance = jnp.abs(key_slab - query_slab)
        before = jnp.where(key_slab < query_slab, 0, 1)
        first = jnp.where(distance == 1, before * n_blocks, HD + key_slab * n_blocks)
        whole = jnp.where(distance == 0, 1.0, 0.0)
        reach = window[distance].astype(F32)
        for j in range(n_blocks):
            picked = jnp.sum(jnp.where(lane == first + j, masks, 0.0), axis=1, keepdims=True)
            limit = jnp.where(jnp.maximum(picked, whole) > 0.5, reach, 0.0)
            for i in range(n_blocks):
                here = jnp.broadcast_to(limit[i : i + 1, :], (BLK, BLK))
                out[c, i * BLK : (i + 1) * BLK, j * BLK : (j + 1) * BLK] = jnp.where(
                    gaps[i - j] < here, 0.0, BARRED
                )


def biases(side, ids, window, queries, n_blocks, before):
    n_slabs = ids.shape[0] - 4
    rows = n_blocks * BLK
    return pl.pallas_call(
        functools.partial(bias_kernel, side, n_slabs, n_blocks),
        in_specs=[IN_SMEM] * 2 + [IN_VMEM] * 2,
        out_specs=IN_VMEM,
        out_shape=jax.ShapeDtypeStruct((n_slabs, rows, rows), F32),
        compiler_params=params(16),
        cost_estimate=cost(0.5),
        name="biases",
    )(ids, window, queries, before)


def attend_body(slabs, packed, heads, bias, queries, chunks, before, out):
    rows = bias.shape[1]
    ones = jnp.ones((rows, HD), BF16)
    if packed:
        out[rows:, :] = jnp.zeros((PAD, out.shape[1]), BF16)
    for h in range(*heads):
        span = slice(h * HD, (h + 1) * HD)
        keys = jnp.concatenate([key[:, span] for key, _ in chunks], axis=0)
        scores = lax.dot_general(
            queries[:rows, span], keys, (((1,), (1,)), ((), ())), preferred_element_type=F32
        )
        weights = [
            jnp.exp(scores[:, n * rows : (n + 1) * rows] + bias[slab]).astype(BF16)
            for n, slab in enumerate(slabs)
        ]
        values = jnp.concatenate(
            [jnp.concatenate([value[:, span], ones], axis=1) for _, value in chunks], axis=0
        )
        sums = jnp.dot(jnp.concatenate(weights, axis=1), values, preferred_element_type=F32)
        if before is not None:
            sums = sums + before[h]
        if not packed:
            out[h] = sums
            continue
        span = slice((h - heads[0]) * HD, (h - heads[0] + 1) * HD)
        out[:rows, span] = sums[:, :HD].astype(BF16)
        for b in range(rows // HD):
            pack_denominator(out, rows, b, span, sums[b * HD : (b + 1) * HD, HD:])


def taken_chunks(lone, rows, refs):
    chunks = []
    for apart in lone:
        if apart:
            keys, values = refs.pop(0), refs.pop(0)
            chunks.append((keys.at[:rows], values.at[values.shape[0] - rows :]))
        else:
            both = refs.pop(0)
            chunks.append((both.at[:rows], both.at[rows:]))
    return chunks


def attend_kernel(slabs, lone, has_totals, heads, bias, queries, _, *refs):
    refs = list(refs)
    chunks = taken_chunks(lone, bias.shape[1], refs)
    before, out = (refs[0], refs[1]) if has_totals else (None, refs[0])
    attend_body(slabs, False, heads, bias, queries, chunks, before, out)


def pair_kernel(slabs, lone, heads, first_bias, first, second_bias, second, *refs):
    refs = list(refs)
    rows = first_bias.shape[1]
    chunks = taken_chunks(lone, rows, refs)
    first_totals, second_totals, out = refs
    held = rows + PAD
    attend_body(slabs, True, heads, first_bias, first, chunks, first_totals, out.at[:held])
    attend_body(slabs, True, heads, second_bias, second, chunks, second_totals, out.at[held:])


def attend_pair(first, second, parts, heads, name):
    rows = first[0].shape[1]
    operands = [first[0], first[1], second[0], second[1]]
    operands += [array for chunk, _ in parts for array in chunk] + [first[2], second[2]]
    return pl.pallas_call(
        functools.partial(
            pair_kernel, [slab for _, slab in parts], [len(c) > 1 for c, _ in parts], heads
        ),
        in_specs=[IN_VMEM] * len(operands),
        out_specs=IN_VMEM,
        out_shape=jax.ShapeDtypeStruct((2 * (rows + PAD), (heads[1] - heads[0]) * HD), BF16),
        compiler_params=params(24),
        cost_estimate=cost(0.6),
        name=name,
    )(*operands)


def attend(bias, queries, before, parts, totals, heads, name):
    rows = bias.shape[1]
    operands = [bias, queries, before] + [array for chunk, _ in parts for array in chunk]
    if totals is not None:
        operands.append(totals)
    count = heads[1] - heads[0]
    shape = jax.ShapeDtypeStruct((count, rows, 2 * HD), F32)
    slabs = [slab for _, slab in parts]
    return pl.pallas_call(
        functools.partial(
            attend_kernel, slabs, [len(c) > 1 for c, _ in parts], totals is not None, heads
        ),
        in_specs=[IN_VMEM] * len(operands),
        out_specs=IN_VMEM,
        out_shape=shape,
        compiler_params=params(24),
        cost_estimate=cost(0.08 * len(parts) * count + 0.15),
        name=name,
    )(*operands)


def packed_sums(packed, first, rows, block, span):
    here = slice(first + block * HD, first + (block + 1) * HD)
    pair = packed[first + rows : first + rows + PAD, span].astype(F32)
    row = pair[2 * block : 2 * block + 1, :] + pair[2 * block + 1 : 2 * block + 2, :]
    return packed[here, span].astype(F32), jnp.broadcast_to(row, (HD, HD)).T


def pack_denominator(out, rows, block, span, denominator):
    row = denominator.T[0:1, :]
    high = row.astype(BF16)
    out[rows + 2 * block : rows + 2 * block + 1, span] = high
    out[rows + 2 * block + 1 : rows + 2 * block + 2, span] = (row - high.astype(F32)).astype(BF16)


def join_kernel(last, firsts, kept, *refs):
    got, out = refs[:-2], refs[-1]
    heads, rows, _ = kept.shape
    if not last:
        out[rows:, :] = jnp.zeros((PAD, out.shape[1]), BF16)
    for h in range(heads):
        span = slice(h * HD, (h + 1) * HD)
        for b in range(rows // HD):
            here = slice(b * HD, (b + 1) * HD)
            num, den = kept[h, here, :HD], kept[h, here, HD:]
            for first, packed in zip(firsts, got):
                more_num, more_den = packed_sums(packed, first, rows, b, span)
                num, den = num + more_num, den + more_den
            if last:
                out[here, span] = (num / den).astype(BF16)
            else:
                out[here, span] = num.astype(BF16)
                pack_denominator(out, rows, b, span, den)


def join(kept, got, last, before):
    heads, rows, _ = kept.shape
    return pl.pallas_call(
        functools.partial(join_kernel, last, [first for _, first in got]),
        in_specs=[IN_VMEM] * (2 + len(got)),
        out_specs=IN_VMEM,
        out_shape=jax.ShapeDtypeStruct((rows + (0 if last else PAD), heads * HD), BF16),
        compiler_params=params(16),
        cost_estimate=cost(0.15),
        name="finish" if last else "join",
    )(kept, *[array for array, _ in got], before)


def gate_kernel(array, _, out):
    pass


def gate(array, before):
    return pl.pallas_call(
        gate_kernel,
        in_specs=[ANYWHERE, IN_VMEM],
        out_specs=ANYWHERE,
        out_shape=jax.ShapeDtypeStruct(array.shape, array.dtype),
        input_output_aliases={0: 0},
        compiler_params=params(16),
        cost_estimate=cost(0.1),
        name="gate",
    )(array, before)


def row_dot(summed, values):
    dots = lax.dot_general(
        summed, values, (((1,), (1,)), ((), ())), preferred_element_type=F32
    )
    return dots[0:1, :] + (dots[1:2, :] + dots[2:3, :])


def early_kernel(n_head, place, own, w_out, sums, received, partial, parts, owners, held):
    cols = partial.shape[1]
    first = pl.multiple_of(place[0] * cols, HD)
    partial[...] = jnp.dot(own[...], w_out[:, pl.ds(first, cols)], preferred_element_type=F32)
    held[...] = received[...]
    parts[...] = jnp.zeros(parts.shape, F32)
    parts[pl.ds(place[0], 1), :] = row_dot(sums[...], own[...])
    row = lax.broadcasted_iota(jnp.int32, parts.shape, 0)
    for k in range(1, n_head):
        owner = lax.rem(place[0] - k + n_head, n_head)
        owners[k - 1] = jnp.where(row == owner, 1.0, 0.0)


def project_early(place, own, w_out, sums, received, n_head):
    rows = own.shape[0]
    cols = w_out.shape[1] // n_head
    places = -(-n_head // 8) * 8
    return pl.pallas_call(
        functools.partial(early_kernel, n_head),
        in_specs=[IN_SMEM] + [IN_VMEM] * 4,
        out_specs=[IN_VMEM] * 4,
        out_shape=[
            jax.ShapeDtypeStruct((rows, cols), F32),
            jax.ShapeDtypeStruct((places, rows), F32),
            jax.ShapeDtypeStruct((n_head - 1, places, rows), F32),
            jax.ShapeDtypeStruct(received.shape, BF16),
        ],
        compiler_params=params(24),
        cost_estimate=cost(1.4),
        name="project_early",
    )(place, own, w_out, sums, received)


def last_kernel(n_head, *refs):
    late, refs = refs[: n_head - 1], refs[n_head - 1 :]
    received, sums, partial, parts, owners, layer_out, checksum, staged, sems = refs
    rows, cols = partial.shape
    tiles = sems.shape[0]
    tile = cols // tiles
    stores = []
    for t in range(tiles):
        here = slice(t * tile, (t + 1) * tile)
        total = partial[:, here]
        for k in range(1, n_head):
            total = total + jnp.dot(
                late[k - 1][...], received[k - 1, :, here], preferred_element_type=F32
            )
        staged[:, here] = total.astype(BF16)
        there = pl.ds(t * tile, tile)
        store = pltpu.make_async_copy(staged.at[:, there], layer_out.at[:, there], sems.at[t])
        store.start()
        stores.append(store)
    every = parts[...]
    for k in range(1, n_head):
        dot = row_dot(sums[(k - 1) * PAD : k * PAD, :], late[k - 1][...])
        every = every + owners[k - 1] * dot
    sum_all = every[0:1, :]
    for k in range(1, n_head):
        sum_all = sum_all + every[k : k + 1, :]
    checksum[...] = sum_all * D ** (-0.5)
    for store in stores:
        store.wait()


def project_last(late, received, sums, partial, parts, owners):
    n_head = len(late) + 1
    rows, cols = partial.shape
    tiles = next(t for t in (3, 2, 1) if cols % (t * HD) == 0)
    operands = [*late, received, sums, partial, parts, owners]
    layer_out, checksum = pl.pallas_call(
        functools.partial(last_kernel, n_head),
        in_specs=[IN_VMEM] * len(operands),
        out_specs=[ANYWHERE, IN_VMEM],
        out_shape=[
            jax.ShapeDtypeStruct((rows, cols), BF16),
            jax.ShapeDtypeStruct((1, rows), F32),
        ],
        scratch_shapes=[VMEM((rows, cols), BF16), pltpu.SemaphoreType.DMA((tiles,))],
        compiler_params=params(24),
        name="project_last",
    )(*operands)
    return layer_out, checksum.reshape(rows)


def per_device(tokens, w_qkv, norm_gains, w_out, near_mask, far_pattern, window):
    rows = tokens.shape[0]
    heads = w_qkv.shape[2] // HD
    n_blocks = rows // BLK
    frame = lax.axis_index("frame").astype(jnp.int32)
    place = lax.axis_index("head").astype(jnp.int32).reshape(1)
    n_frame = lax.axis_size("frame")
    n_head = lax.axis_size("head")
    half = n_frame // 2
    every = (0, heads)

    def swapped(array, by):
        return lax.ppermute(array, "frame", [(i, i ^ by) for i in range(n_frame)])

    def from_head(array, k):
        return lax.ppermute(array, "head", [(i, (i + k) % n_head) for i in range(n_head)])

    def from_heads(arrays):
        got = [from_head(array, k) for k, array in enumerate(arrays, 1)]
        return got[0] if len(got) == 1 else jnp.concatenate(got)

    spans = []
    by = half // 2
    while by > 1:
        spans.append(by)
        by //= 2
    far = sorted((o for o in range(2, half, 2) if o not in spans), key=lambda o: bin(o).count("1"))
    slabs = [0] + spans + far
    n_near = 1 + len(spans)

    kv, queries, payload = project(
        tokens, w_qkv, norm_gains, near_mask, far_pattern, w_out, n_head
    )
    near = {by: swapped(kv, by) for by in spans}
    sib_queries = swapped(queries, 1)
    ids = jnp.stack([frame ^ o for o in [0, 1, half, half ^ 1] + slabs])

    def bias_of(side, array, before):
        return biases(side, ids, window, array, n_blocks, before)

    mine = [((kv,), 0)]
    own_bias = bias_of(0, queries, queries)
    own = attend(own_bias, queries, own_bias, mine, None, every, "attend_first")
    other_queries = swapped(gate(queries, own), half)
    payload = gate(payload, own)
    received = from_heads([payload[k - 1 : k] for k in range(1, n_head)])
    sib_bias = bias_of(1, sib_queries, own)
    sib = attend(sib_bias, sib_queries, sib_bias, mine, None, every, "sibling_first")

    low = spans[-1]
    near[low] = gate(near[low], sib)
    for by in spans[:-1]:
        near[by] = gate(near[by], near[low])
    margin = 2 * PAD
    keys = {by: near[by][: rows + margin] for by in spans}
    values = {by: near[by][rows - margin :] for by in spans}
    for o in far:
        bits = [by for by in spans if o & by]
        values[o] = swapped(values[o ^ bits[0]], bits[0])
        keys[o] = swapped(keys[o ^ bits[-1]], bits[-1])
    early = [((near[by],), i) for i, by in enumerate(spans, 1)]
    sib = attend(sib_bias, sib_queries, sib_bias, early, sib, every, "sibling_second")
    own = attend(own_bias, queries, sib, early, own, every, "attend_second")
    other_bias = bias_of(2, other_queries, own)
    other_queries = gate(other_queries, other_bias)
    other_sib = swapped(other_queries, 1)
    early = [((near[by],), i) for i, by in enumerate(spans, 1)]
    other = attend(
        other_bias, other_queries, other_bias, mine + early, None, every, "other_first"
    )
    other_sib_bias = bias_of(3, other_sib, other)
    both = attend(other_sib_bias, other_sib, other, mine + early, None, every, "other_sibling_first")
    late = []
    for i, o in enumerate(far, n_near):
        late.append(((gate(keys[o], both), gate(values[o], both)), i))
    across = attend_pair(
        (other_sib_bias, other_sib, both), (sib_bias, sib_queries, sib), late, every, "attend_pair"
    )
    other = attend(other_bias, other_queries, across, late, other, every, "other_last")
    own = attend(own_bias, queries, other, late, own, every, "attend_last")
    from_core = swapped(across, 1)
    sent = join(other, [(from_core, 0)], False, own)
    got = swapped(sent, half)
    sums = row_sums(w_out, sent)
    done = join(own, [(from_core, rows + PAD), (got, 0)], True, sums)
    other_sums = from_heads([sums] * (n_head - 1))
    late = [from_head(done, k) for k in range(1, n_head)]
    partial, sum_parts, owners, received = project_early(
        place, done, w_out, sums, received, n_head
    )
    return project_last(late, received, other_sums, partial, sum_parts, owners)


def solution(mesh):
    in_specs = (
        P("frame", None),
        P(None, None, "head"),
        P(None, "head"),
        P("head", None),
        P("frame", None),
        P("frame", None),
        P(),
    )
    out_specs = (P("frame", "head"), P("frame"))
    return jax.shard_map(
        per_device, mesh=mesh, in_specs=in_specs, out_specs=out_specs, check_vma=False
    )
```

```python
import functools

import jax
import jax.numpy as jnp
from jax import lax
from jax.experimental import pallas as pl
from jax.experimental.pallas import tpu as pltpu
from jax.sharding import PartitionSpec as P

D = 3072
HD = 128
BLK = 128
EPS = 1e-06
PAD = 16
BARRED = -1e30
F32 = jnp.float32
BF16 = jnp.bfloat16
VMEM = pltpu.VMEM
SMEM = pltpu.SMEM
MIB = 1024 * 1024
IN_VMEM = pl.BlockSpec(memory_space=VMEM)
IN_SMEM = pl.BlockSpec(memory_space=SMEM)
IN_HBM = pl.BlockSpec(memory_space=pltpu.HBM)
ANYWHERE = pl.BlockSpec(memory_space=pl.ANY)


def params(mib):
    return pltpu.CompilerParams(vmem_limit_bytes=mib * MIB)


def cost(microseconds):
    return pl.CostEstimate(
        flops=int(microseconds * 0), bytes_accessed=int(microseconds * 0), transcendentals=0
    )


def normed(values, gains, scale):
    parts = []
    for first in range(0, values.shape[1], HD):
        head = values[:, first : first + HD]
        factor = lax.rsqrt(jnp.mean(head * head, axis=-1, keepdims=True) + EPS)
        parts.append(head * factor * gains[:, first : first + HD] * scale)
    return jnp.concatenate(parts, axis=1)


def project_kernel(steps, tokens, w_qkv, gains, near_mask, far_pattern, kv, queries, *scratch):
    token_buf, w_buf, gain_buf, near_buf, far_buf, total, sems, small_sems = scratch
    rows, width = tokens.shape
    count, _, cols = w_qkv.shape
    deep = width // steps
    copies = []
    for s in range(steps):
        span = pl.ds(s * deep, deep)
        group = [pltpu.make_async_copy(tokens.at[:, span], token_buf.at[:, span], sems.at[0, s])]
        for j in range(count):
            group.append(
                pltpu.make_async_copy(
                    w_qkv.at[j, span], w_buf.at[span, pl.ds(j * cols, cols)], sems.at[1 + j, s]
                )
            )
        for copy in group:
            copy.start()
        copies.append(group)
    small = [
        pltpu.make_async_copy(source, target, small_sems.at[i])
        for i, (source, target) in enumerate(
            ((gains, gain_buf), (near_mask, near_buf), (far_pattern, far_buf))
        )
    ]
    for copy in small:
        copy.start()
    for s in range(steps):
        for copy in copies[s]:
            copy.wait()
        span = slice(s * deep, (s + 1) * deep)
        part = jnp.dot(token_buf[:, span], w_buf[span, :], preferred_element_type=F32)
        if s == 0:
            total[...] = part
        elif s < steps - 1:
            total[...] += part
    part = total[...] + part
    for copy in small:
        copy.wait()
    query, key, value = (part[:, j * cols : (j + 1) * cols] for j in range(count))
    kv[:rows, :] = normed(key, gain_buf[1:2, :], 1.0).astype(BF16)
    kv[rows:, :] = value.astype(BF16)
    queries[:rows, :] = normed(query, gain_buf[0:1, :], HD ** (-0.5)).astype(BF16)
    n_blocks, n_near = near_mask.shape
    queries[rows:, :] = jnp.zeros((PAD, cols), BF16)
    queries[rows : rows + n_blocks, :n_near] = near_buf[...].astype(F32).astype(BF16)
    queries[rows : rows + n_blocks, HD : HD + far_pattern.shape[1]] = (
        far_buf[...].astype(F32).astype(BF16)
    )


def project(tokens, w_qkv, gains, near_mask, far_pattern):
    rows, width = tokens.shape
    count, _, cols = w_qkv.shape
    steps = 4
    return pl.pallas_call(
        functools.partial(project_kernel, steps),
        in_specs=[ANYWHERE] * 5,
        out_specs=[IN_VMEM] * 2,
        out_shape=[
            jax.ShapeDtypeStruct((2 * rows, cols), BF16),
            jax.ShapeDtypeStruct((rows + PAD, cols), BF16),
        ],
        scratch_shapes=[
            VMEM((rows, width), BF16),
            VMEM((width, count * cols), BF16),
            VMEM(gains.shape, F32),
            VMEM(near_mask.shape, jnp.int32),
            VMEM(far_pattern.shape, jnp.int32),
            VMEM((rows, count * cols), F32),
            pltpu.SemaphoreType.DMA((1 + count, steps)),
            pltpu.SemaphoreType.DMA((3,)),
        ],
        compiler_params=params(56),
        cost_estimate=cost(5.0),
        name="project",
    )(tokens, w_qkv, gains, near_mask, far_pattern)


def split_sum(values):
    high = values.astype(BF16).astype(F32)
    mid = (values - high).astype(BF16).astype(F32)
    return high, mid, values - high - mid


def columns_kernel(n_head, w_out, _, payload, sems):
    cols = payload.shape[2]
    place = lax.axis_index("head")
    copies = []
    for k in range(1, n_head):
        first = pl.multiple_of(lax.rem(place + k, n_head) * cols, HD)
        copies.append(
            pltpu.make_async_copy(w_out.at[:, pl.ds(first, cols)], payload.at[k - 1], sems.at[k - 1])
        )
    for copy in copies:
        copy.start()
    for copy in copies:
        copy.wait()


def columns_of(w_out, n_head, before):
    rows, width = w_out.shape
    return pl.pallas_call(
        functools.partial(columns_kernel, n_head),
        in_specs=[ANYWHERE, IN_VMEM],
        out_specs=IN_VMEM,
        out_shape=jax.ShapeDtypeStruct((n_head - 1, rows, width // n_head), BF16),
        scratch_shapes=[pltpu.SemaphoreType.DMA((n_head - 1,))],
        compiler_params=params(16),
        cost_estimate=cost(1.0),
        name="columns",
    )(w_out, before)


def sums_kernel(w_out, _, sums):
    rows, width = w_out.shape
    total = lax.dot_general(
        jnp.ones((8, width), BF16), w_out[...], (((1,), (1,)), ((), ())), preferred_element_type=F32
    )
    high, mid, low = split_sum(total)
    row = lax.broadcasted_iota(jnp.int32, (8, rows), 0)
    packed = jnp.where(row == 0, high, jnp.where(row == 1, mid, jnp.where(row == 2, low, 0.0)))
    sums[...] = jnp.concatenate([packed, jnp.zeros((PAD - 8, rows), F32)], axis=0).astype(BF16)


def row_sums(w_out, before):
    return pl.pallas_call(
        sums_kernel,
        in_specs=[IN_VMEM] * 2,
        out_specs=IN_VMEM,
        out_shape=jax.ShapeDtypeStruct((PAD, w_out.shape[0]), BF16),
        compiler_params=params(16),
        cost_estimate=cost(0.8),
        name="row_sums",
    )(w_out, before)


def bias_kernel(side, n_slabs, n_blocks, ids, window, queries, _, out):
    rows = n_blocks * BLK
    shifted = lax.broadcasted_iota(jnp.int32, (BLK, BLK), 0) - lax.broadcasted_iota(
        jnp.int32, (BLK, BLK), 1
    )
    gaps = {
        by: jnp.abs(shifted + by * BLK).astype(F32) for by in range(1 - n_blocks, n_blocks)
    }
    lane = lax.broadcasted_iota(jnp.int32, (PAD, queries.shape[1]), 1)
    masks = queries[rows : rows + PAD, :].astype(F32)
    query_slab = ids[side]
    for c in range(n_slabs):
        key_slab = ids[4 + c]
        distance = jnp.abs(key_slab - query_slab)
        before = jnp.where(key_slab < query_slab, 0, 1)
        first = jnp.where(distance == 1, before * n_blocks, HD + key_slab * n_blocks)
        whole = jnp.where(distance == 0, 1.0, 0.0)
        reach = window[distance].astype(F32)
        for j in range(n_blocks):
            picked = jnp.sum(jnp.where(lane == first + j, masks, 0.0), axis=1, keepdims=True)
            limit = jnp.where(jnp.maximum(picked, whole) > 0.5, reach, 0.0)
            for i in range(n_blocks):
                here = jnp.broadcast_to(limit[i : i + 1, :], (BLK, BLK))
                out[c, i * BLK : (i + 1) * BLK, j * BLK : (j + 1) * BLK] = jnp.where(
                    gaps[i - j] < here, 0.0, BARRED
                )


def table_kernel(sides, n_slabs, n_blocks, ids, window, _, *tables):
    for side, table in zip(sides, tables):
        lanes, cols = table.shape
        lane = lax.broadcasted_iota(jnp.int32, (lanes, cols), 0)
        col = lax.broadcasted_iota(jnp.int32, (lanes, cols), 1)
        value = jnp.zeros((lanes, cols), F32)
        query_slab = ids[side]
        for c in range(n_slabs):
            key_slab = ids[4 + c]
            distance = jnp.abs(key_slab - query_slab)
            before = jnp.where(key_slab < query_slab, 0, 1)
            first = jnp.where(distance == 1, before * n_blocks, HD + key_slab * n_blocks)
            reach = window[distance].astype(F32)
            here = (lane - first == col - c * n_blocks) & (col // n_blocks == c)
            value = jnp.where(here, reach, value)
        table[...] = value.astype(BF16)


def tables(sides, ids, window, lanes, n_blocks, before):
    n_slabs = ids.shape[0] - 4
    return pl.pallas_call(
        functools.partial(table_kernel, sides, n_slabs, n_blocks),
        in_specs=[IN_SMEM] * 2 + [IN_VMEM],
        out_specs=[IN_VMEM] * len(sides),
        out_shape=[jax.ShapeDtypeStruct((lanes, HD), BF16) for _ in sides],
        compiler_params=params(16),
        cost_estimate=cost(0.5),
        name="tables",
    )(ids, window, before)


def late_bias_kernel(n_slabs, n_blocks, table, queries, _, out):
    rows = n_blocks * BLK
    limits = jnp.dot(queries[rows : rows + PAD, :], table[...], preferred_element_type=F32)
    shifted = lax.broadcasted_iota(jnp.int32, (BLK, BLK), 0) - lax.broadcasted_iota(
        jnp.int32, (BLK, BLK), 1
    )
    gaps = {
        by: jnp.abs(shifted + by * BLK).astype(F32) for by in range(1 - n_blocks, n_blocks)
    }
    for c in range(n_slabs):
        for i in range(n_blocks):
            for j in range(n_blocks):
                at = c * n_blocks + j
                here = jnp.broadcast_to(limits[i : i + 1, at : at + 1], (BLK, BLK))
                out[c, i * BLK : (i + 1) * BLK, j * BLK : (j + 1) * BLK] = jnp.where(
                    gaps[i - j] < here, 0.0, BARRED
                )


def late_biases(table, queries, n_slabs, n_blocks, before):
    rows = n_blocks * BLK
    return pl.pallas_call(
        functools.partial(late_bias_kernel, n_slabs, n_blocks),
        in_specs=[IN_VMEM] * 3,
        out_specs=IN_VMEM,
        out_shape=jax.ShapeDtypeStruct((n_slabs, rows, rows), F32),
        compiler_params=params(16),
        cost_estimate=cost(0.3),
        name="late_biases",
    )(table, queries, before)


def biases(side, ids, window, queries, n_blocks, before):
    n_slabs = ids.shape[0] - 4
    rows = n_blocks * BLK
    return pl.pallas_call(
        functools.partial(bias_kernel, side, n_slabs, n_blocks),
        in_specs=[IN_SMEM] * 2 + [IN_VMEM] * 2,
        out_specs=IN_VMEM,
        out_shape=jax.ShapeDtypeStruct((n_slabs, rows, rows), F32),
        compiler_params=params(16),
        cost_estimate=cost(0.5),
        name="biases",
    )(ids, window, queries, before)


def attend_body(slabs, packed, heads, bias, queries, chunks, before, out):
    rows = bias.shape[1]
    ones = jnp.ones((rows, HD), BF16)
    if packed:
        out[rows:, :] = jnp.zeros((PAD, out.shape[1]), BF16)
    for h in range(*heads):
        span = slice(h * HD, (h + 1) * HD)
        keys = jnp.concatenate([key[:, span] for key, _ in chunks], axis=0)
        scores = lax.dot_general(
            queries[:rows, span], keys, (((1,), (1,)), ((), ())), preferred_element_type=F32
        )
        weights = [
            jnp.exp(scores[:, n * rows : (n + 1) * rows] + bias[slab]).astype(BF16)
            for n, slab in enumerate(slabs)
        ]
        values = jnp.concatenate(
            [jnp.concatenate([value[:, span], ones], axis=1) for _, value in chunks], axis=0
        )
        sums = jnp.dot(jnp.concatenate(weights, axis=1), values, preferred_element_type=F32)
        if before is not None:
            sums = sums + before[h]
        if not packed:
            out[h] = sums
            continue
        span = slice((h - heads[0]) * HD, (h - heads[0] + 1) * HD)
        out[:rows, span] = sums[:, :HD].astype(BF16)
        for b in range(rows // HD):
            pack_denominator(out, rows, b, span, sums[b * HD : (b + 1) * HD, HD:])


def taken_chunks(lone, rows, refs):
    chunks = []
    for apart in lone:
        if apart:
            keys, values = refs.pop(0), refs.pop(0)
            chunks.append((keys.at[:rows], values.at[values.shape[0] - rows :]))
        else:
            both = refs.pop(0)
            chunks.append((both.at[:rows], both.at[rows:]))
    return chunks


def attend_kernel(slabs, lone, has_totals, heads, bias, queries, _, *refs):
    refs = list(refs)
    chunks = taken_chunks(lone, bias.shape[1], refs)
    before, out = (refs[0], refs[1]) if has_totals else (None, refs[0])
    attend_body(slabs, False, heads, bias, queries, chunks, before, out)


def pair_kernel(slabs, lone, heads, first_bias, first, second_bias, second, *refs):
    refs = list(refs)
    rows = first_bias.shape[1]
    chunks = taken_chunks(lone, rows, refs)
    first_totals, second_totals, out = refs
    held = rows + PAD
    attend_body(slabs, True, heads, first_bias, first, chunks, first_totals, out.at[:held])
    attend_body(slabs, True, heads, second_bias, second, chunks, second_totals, out.at[held:])


def attend_pair(first, second, parts, heads, name):
    rows = first[0].shape[1]
    operands = [first[0], first[1], second[0], second[1]]
    operands += [array for chunk, _ in parts for array in chunk] + [first[2], second[2]]
    return pl.pallas_call(
        functools.partial(
            pair_kernel, [slab for _, slab in parts], [len(c) > 1 for c, _ in parts], heads
        ),
        in_specs=[IN_VMEM] * len(operands),
        out_specs=IN_VMEM,
        out_shape=jax.ShapeDtypeStruct((2 * (rows + PAD), (heads[1] - heads[0]) * HD), BF16),
        compiler_params=params(24),
        cost_estimate=cost(0.6),
        name=name,
    )(*operands)


def attend(bias, queries, before, parts, totals, heads, name):
    rows = bias.shape[1]
    operands = [bias, queries, before] + [array for chunk, _ in parts for array in chunk]
    if totals is not None:
        operands.append(totals)
    count = heads[1] - heads[0]
    shape = jax.ShapeDtypeStruct((count, rows, 2 * HD), F32)
    slabs = [slab for _, slab in parts]
    return pl.pallas_call(
        functools.partial(
            attend_kernel, slabs, [len(c) > 1 for c, _ in parts], totals is not None, heads
        ),
        in_specs=[IN_VMEM] * len(operands),
        out_specs=IN_VMEM,
        out_shape=shape,
        compiler_params=params(24),
        cost_estimate=cost(0.08 * len(parts) * count + 0.15),
        name=name,
    )(*operands)


def packed_sums(packed, first, rows, block, span):
    here = slice(first + block * HD, first + (block + 1) * HD)
    pair = packed[first + rows : first + rows + PAD, span].astype(F32)
    row = pair[2 * block : 2 * block + 1, :] + pair[2 * block + 1 : 2 * block + 2, :]
    return packed[here, span].astype(F32), jnp.broadcast_to(row, (HD, HD)).T


def pack_denominator(out, rows, block, span, denominator):
    row = denominator.T[0:1, :]
    high = row.astype(BF16)
    out[rows + 2 * block : rows + 2 * block + 1, span] = high
    out[rows + 2 * block + 1 : rows + 2 * block + 2, span] = (row - high.astype(F32)).astype(BF16)


def join_kernel(last, firsts, kept, *refs):
    got, out = refs[:-2], refs[-1]
    heads, rows, _ = kept.shape
    if not last:
        out[rows:, :] = jnp.zeros((PAD, out.shape[1]), BF16)
    for h in range(heads):
        span = slice(h * HD, (h + 1) * HD)
        for b in range(rows // HD):
            here = slice(b * HD, (b + 1) * HD)
            num, den = kept[h, here, :HD], kept[h, here, HD:]
            for first, packed in zip(firsts, got):
                more_num, more_den = packed_sums(packed, first, rows, b, span)
                num, den = num + more_num, den + more_den
            if last:
                out[here, span] = (num / den).astype(BF16)
            else:
                out[here, span] = num.astype(BF16)
                pack_denominator(out, rows, b, span, den)


def join(kept, got, last, before):
    heads, rows, _ = kept.shape
    return pl.pallas_call(
        functools.partial(join_kernel, last, [first for _, first in got]),
        in_specs=[IN_VMEM] * (2 + len(got)),
        out_specs=IN_VMEM,
        out_shape=jax.ShapeDtypeStruct((rows + (0 if last else PAD), heads * HD), BF16),
        compiler_params=params(16),
        cost_estimate=cost(0.15),
        name="finish" if last else "join",
    )(kept, *[array for array, _ in got], before)


def gate_kernel(array, _, out):
    pass


def copy_kernel(array, _, out):
    out[...] = array[...]


def copied(array, before):
    return pl.pallas_call(
        copy_kernel,
        in_specs=[IN_VMEM] * 2,
        out_specs=IN_VMEM,
        out_shape=jax.ShapeDtypeStruct(array.shape, array.dtype),
        compiler_params=params(16),
        cost_estimate=cost(0.1),
        name="copied",
    )(array, before)


def gate(array, before):
    return pl.pallas_call(
        gate_kernel,
        in_specs=[IN_VMEM] * 2,
        out_specs=IN_VMEM,
        out_shape=jax.ShapeDtypeStruct(array.shape, array.dtype),
        input_output_aliases={0: 0},
        compiler_params=params(16),
        cost_estimate=cost(0.1),
        name="gate",
    )(array, before)


def row_dot(summed, values):
    dots = lax.dot_general(
        summed, values, (((1,), (1,)), ((), ())), preferred_element_type=F32
    )
    return dots[0:1, :] + (dots[1:2, :] + dots[2:3, :])


def early_kernel(n_head, place, own, w_out, sums, received, partial, parts, owners, held):
    cols = partial.shape[1]
    first = pl.multiple_of(place[0] * cols, HD)
    partial[...] = jnp.dot(own[...], w_out[:, pl.ds(first, cols)], preferred_element_type=F32)
    held[...] = received[...]
    parts[...] = jnp.zeros(parts.shape, F32)
    parts[pl.ds(place[0], 1), :] = row_dot(sums[...], own[...])
    row = lax.broadcasted_iota(jnp.int32, parts.shape, 0)
    for k in range(1, n_head):
        owner = lax.rem(place[0] - k + n_head, n_head)
        owners[k - 1] = jnp.where(row == owner, 1.0, 0.0)


def project_early(place, own, w_out, sums, received, n_head):
    rows = own.shape[0]
    cols = w_out.shape[1] // n_head
    places = -(-n_head // 8) * 8
    return pl.pallas_call(
        functools.partial(early_kernel, n_head),
        in_specs=[IN_SMEM] + [IN_VMEM] * 4,
        out_specs=[IN_VMEM] * 4,
        out_shape=[
            jax.ShapeDtypeStruct((rows, cols), F32),
            jax.ShapeDtypeStruct((places, rows), F32),
            jax.ShapeDtypeStruct((n_head - 1, places, rows), F32),
            jax.ShapeDtypeStruct(received.shape, BF16),
        ],
        compiler_params=params(24),
        cost_estimate=cost(1.4),
        name="project_early",
    )(place, own, w_out, sums, received)


def last_kernel(n_head, *refs):
    late, refs = refs[: n_head - 1], refs[n_head - 1 :]
    received, sums, partial, parts, owners, layer_out, checksum, staged, sems = refs
    rows, cols = partial.shape
    tiles = sems.shape[0]
    tile = cols // tiles
    stores = []
    for t in range(tiles):
        here = slice(t * tile, (t + 1) * tile)
        total = partial[:, here]
        for k in range(1, n_head):
            total = total + jnp.dot(
                late[k - 1][...], received[k - 1, :, here], preferred_element_type=F32
            )
        staged[:, here] = total.astype(BF16)
        there = pl.ds(t * tile, tile)
        store = pltpu.make_async_copy(staged.at[:, there], layer_out.at[:, there], sems.at[t])
        store.start()
        stores.append(store)
    every = parts[...]
    for k in range(1, n_head):
        dot = row_dot(sums[(k - 1) * PAD : k * PAD, :], late[k - 1][...])
        every = every + owners[k - 1] * dot
    sum_all = every[0:1, :]
    for k in range(1, n_head):
        sum_all = sum_all + every[k : k + 1, :]
    checksum[...] = sum_all * D ** (-0.5)
    for store in stores:
        store.wait()


def project_last(late, received, sums, partial, parts, owners):
    n_head = len(late) + 1
    rows, cols = partial.shape
    tiles = next(t for t in (3, 2, 1) if cols % (t * HD) == 0)
    operands = [*late, received, sums, partial, parts, owners]
    layer_out, checksum = pl.pallas_call(
        functools.partial(last_kernel, n_head),
        in_specs=[IN_VMEM] * len(operands),
        out_specs=[ANYWHERE, IN_VMEM],
        out_shape=[
            jax.ShapeDtypeStruct((rows, cols), BF16),
            jax.ShapeDtypeStruct((1, rows), F32),
        ],
        scratch_shapes=[VMEM((rows, cols), BF16), pltpu.SemaphoreType.DMA((tiles,))],
        compiler_params=params(24),
        name="project_last",
    )(*operands)
    return layer_out, checksum.reshape(rows)


def per_device(tokens, w_qkv, norm_gains, w_out, near_mask, far_pattern, window):
    rows = tokens.shape[0]
    heads = w_qkv.shape[2] // HD
    n_blocks = rows // BLK
    frame = lax.axis_index("frame").astype(jnp.int32)
    place = lax.axis_index("head").astype(jnp.int32).reshape(1)
    n_frame = lax.axis_size("frame")
    n_head = lax.axis_size("head")
    half = n_frame // 2
    every = (0, heads)

    def swapped(array, by):
        return lax.ppermute(array, "frame", [(i, i ^ by) for i in range(n_frame)])

    def from_head(array, k):
        return lax.ppermute(array, "head", [(i, (i + k) % n_head) for i in range(n_head)])

    def from_heads(arrays):
        got = [from_head(array, k) for k, array in enumerate(arrays, 1)]
        return got[0] if len(got) == 1 else jnp.concatenate(got)

    spans = []
    by = half // 2
    while by > 1:
        spans.append(by)
        by //= 2
    far = sorted((o for o in range(2, half, 2) if o not in spans), key=lambda o: bin(o).count("1"))
    slabs = [0] + spans + far
    n_near = 1 + len(spans)

    kv, queries = project(tokens, w_qkv, norm_gains, near_mask, far_pattern)
    near = {by: swapped(kv, by) for by in spans}
    sib_queries = swapped(queries, 1)
    ids = jnp.stack([frame ^ o for o in [0, 1, half, half ^ 1] + slabs])

    def bias_of(side, array, before):
        return biases(side, ids, window, array, n_blocks, before)

    mine = [((kv,), 0)]
    own_bias = bias_of(0, queries, queries)
    own = attend(own_bias, queries, own_bias, mine, None, every, "attend_first")
    other_queries = swapped(copied(queries, own), half)
    payload = columns_of(w_out, n_head, own)
    received = from_heads([payload[k - 1 : k] for k in range(1, n_head)])
    other_table, other_sib_table = tables(
        (2, 3), ids, window, queries.shape[1], n_blocks, own
    )
    sib_bias = bias_of(1, sib_queries, other_sib_table)
    sib = attend(sib_bias, sib_queries, sib_bias, mine, None, every, "sibling_first")

    before = sib
    for by in spans:
        near[by] = before = gate(near[by], before)
    margin = 2 * PAD
    keys = {by: near[by][: rows + margin] for by in spans}
    values = {by: near[by][rows - margin :] for by in spans}
    for o in far:
        bits = [by for by in spans if o & by]
        values[o] = swapped(values[o ^ bits[0]], bits[0])
        keys[o] = swapped(keys[o ^ bits[-1]], bits[-1])
    early = [((near[by],), i) for i, by in enumerate(spans, 1)]
    sib = attend(sib_bias, sib_queries, sib_bias, early, sib, every, "sibling_second")
    own = attend(own_bias, queries, sib, early, own, every, "attend_second")
    other_bias = late_biases(other_table, other_queries, len(slabs), n_blocks, own)
    other_queries = gate(other_queries, other_bias)
    other_sib = swapped(other_queries, 1)
    early = [((near[by],), i) for i, by in enumerate(spans, 1)]
    other = attend(
        other_bias, other_queries, other_bias, mine + early, None, every, "other_first"
    )
    other_sib_bias = late_biases(other_sib_table, other_sib, len(slabs), n_blocks, other)
    both = attend(other_sib_bias, other_sib, other, mine + early, None, every, "other_sibling_first")
    late = []
    for i, o in enumerate(far, n_near):
        late.append(((gate(keys[o], both), gate(values[o], both)), i))
    across = attend_pair(
        (other_sib_bias, other_sib, both), (sib_bias, sib_queries, sib), late, every, "attend_pair"
    )
    other = attend(other_bias, other_queries, across, late, other, every, "other_last")
    own = attend(own_bias, queries, other, late, own, every, "attend_last")
    from_core = swapped(across, 1)
    sent = join(other, [(from_core, 0)], False, own)
    got = swapped(sent, half)
    sums = row_sums(w_out, sent)
    done = join(own, [(from_core, rows + PAD), (got, 0)], True, sums)
    other_sums = from_heads([sums] * (n_head - 1))
    late = [from_head(done, k) for k in range(1, n_head)]
    partial, sum_parts, owners, received = project_early(
        place, done, w_out, sums, received, n_head
    )
    return project_last(late, received, other_sums, partial, sum_parts, owners)


def solution(mesh):
    in_specs = (
        P("frame", None),
        P(None, None, "head"),
        P(None, "head"),
        P("head", None),
        P("frame", None),
        P("frame", None),
        P(),
    )
    out_specs = (P("frame", "head"), P("frame"))
    return jax.shard_map(
        per_device, mesh=mesh, in_specs=in_specs, out_specs=out_specs, check_vma=False
    )
```

```python
import functools

import jax
import jax.numpy as jnp
from jax import lax
from jax.experimental import pallas as pl
from jax.experimental.pallas import tpu as pltpu
from jax.sharding import PartitionSpec as P

D = 3072
HD = 128
BLK = 128
EPS = 1e-06
PAD = 16
BARRED = -1e30
F32 = jnp.float32
BF16 = jnp.bfloat16
VMEM = pltpu.VMEM
SMEM = pltpu.SMEM
MIB = 1024 * 1024
IN_VMEM = pl.BlockSpec(memory_space=VMEM)
IN_SMEM = pl.BlockSpec(memory_space=SMEM)
IN_HBM = pl.BlockSpec(memory_space=pltpu.HBM)
ANYWHERE = pl.BlockSpec(memory_space=pl.ANY)


def params(mib):
    return pltpu.CompilerParams(vmem_limit_bytes=mib * MIB)


def cost(microseconds):
    return pl.CostEstimate(
        flops=int(microseconds * 0), bytes_accessed=int(microseconds * 0), transcendentals=0
    )


def normed(values, gains, scale):
    parts = []
    for first in range(0, values.shape[1], HD):
        head = values[:, first : first + HD]
        factor = lax.rsqrt(jnp.mean(head * head, axis=-1, keepdims=True) + EPS)
        parts.append(head * factor * gains[:, first : first + HD] * scale)
    return jnp.concatenate(parts, axis=1)


def project_kernel(steps, tokens, w_qkv, gains, near_mask, far_pattern, kv, queries, *scratch):
    token_buf, w_buf, gain_buf, near_buf, far_buf, total, sems, small_sems = scratch
    rows, width = tokens.shape
    count, _, cols = w_qkv.shape
    deep = width // steps
    copies = []
    for s in range(steps):
        span = pl.ds(s * deep, deep)
        group = [pltpu.make_async_copy(tokens.at[:, span], token_buf.at[:, span], sems.at[0, s])]
        for j in range(count):
            group.append(
                pltpu.make_async_copy(
                    w_qkv.at[j, span], w_buf.at[span, pl.ds(j * cols, cols)], sems.at[1 + j, s]
                )
            )
        for copy in group:
            copy.start()
        copies.append(group)
    small = [
        pltpu.make_async_copy(source, target, small_sems.at[i])
        for i, (source, target) in enumerate(
            ((gains, gain_buf), (near_mask, near_buf), (far_pattern, far_buf))
        )
    ]
    for copy in small:
        copy.start()
    for s in range(steps):
        for copy in copies[s]:
            copy.wait()
        span = slice(s * deep, (s + 1) * deep)
        part = jnp.dot(token_buf[:, span], w_buf[span, :], preferred_element_type=F32)
        if s == 0:
            total[...] = part
        elif s < steps - 1:
            total[...] += part
    part = total[...] + part
    for copy in small:
        copy.wait()
    query, key, value = (part[:, j * cols : (j + 1) * cols] for j in range(count))
    kv[:rows, :] = normed(key, gain_buf[1:2, :], 1.0).astype(BF16)
    kv[rows:, :] = value.astype(BF16)
    queries[:rows, :] = normed(query, gain_buf[0:1, :], HD ** (-0.5)).astype(BF16)
    n_blocks, n_near = near_mask.shape
    queries[rows:, :] = jnp.zeros((PAD, cols), BF16)
    queries[rows : rows + n_blocks, :n_near] = near_buf[...].astype(F32).astype(BF16)
    queries[rows : rows + n_blocks, HD : HD + far_pattern.shape[1]] = (
        far_buf[...].astype(F32).astype(BF16)
    )


def project(tokens, w_qkv, gains, near_mask, far_pattern):
    rows, width = tokens.shape
    count, _, cols = w_qkv.shape
    steps = 4
    return pl.pallas_call(
        functools.partial(project_kernel, steps),
        in_specs=[ANYWHERE] * 5,
        out_specs=[IN_VMEM] * 2,
        out_shape=[
            jax.ShapeDtypeStruct((2 * rows, cols), BF16),
            jax.ShapeDtypeStruct((rows + PAD, cols), BF16),
        ],
        scratch_shapes=[
            VMEM((rows, width), BF16),
            VMEM((width, count * cols), BF16),
            VMEM(gains.shape, F32),
            VMEM(near_mask.shape, jnp.int32),
            VMEM(far_pattern.shape, jnp.int32),
            VMEM((rows, count * cols), F32),
            pltpu.SemaphoreType.DMA((1 + count, steps)),
            pltpu.SemaphoreType.DMA((3,)),
        ],
        compiler_params=params(56),
        cost_estimate=cost(5.0),
        name="project",
    )(tokens, w_qkv, gains, near_mask, far_pattern)


def split_sum(values):
    high = values.astype(BF16).astype(F32)
    mid = (values - high).astype(BF16).astype(F32)
    return high, mid, values - high - mid


def columns_kernel(n_head, w_out, _, payload, sems):
    cols = payload.shape[2]
    place = lax.axis_index("head")
    copies = []
    for k in range(1, n_head):
        first = pl.multiple_of(lax.rem(place + k, n_head) * cols, HD)
        copies.append(
            pltpu.make_async_copy(w_out.at[:, pl.ds(first, cols)], payload.at[k - 1], sems.at[k - 1])
        )
    for copy in copies:
        copy.start()
    for copy in copies:
        copy.wait()


def columns_of(w_out, n_head, before):
    rows, width = w_out.shape
    return pl.pallas_call(
        functools.partial(columns_kernel, n_head),
        in_specs=[ANYWHERE, IN_VMEM],
        out_specs=IN_VMEM,
        out_shape=jax.ShapeDtypeStruct((n_head - 1, rows, width // n_head), BF16),
        scratch_shapes=[pltpu.SemaphoreType.DMA((n_head - 1,))],
        compiler_params=params(16),
        cost_estimate=cost(1.0),
        name="columns",
    )(w_out, before)


def sums_kernel(w_out, _, sums):
    rows, width = w_out.shape
    total = lax.dot_general(
        jnp.ones((8, width), BF16), w_out[...], (((1,), (1,)), ((), ())), preferred_element_type=F32
    )
    high, mid, low = split_sum(total)
    row = lax.broadcasted_iota(jnp.int32, (8, rows), 0)
    packed = jnp.where(row == 0, high, jnp.where(row == 1, mid, jnp.where(row == 2, low, 0.0)))
    sums[...] = jnp.concatenate([packed, jnp.zeros((PAD - 8, rows), F32)], axis=0).astype(BF16)


def row_sums(w_out, before):
    return pl.pallas_call(
        sums_kernel,
        in_specs=[IN_VMEM] * 2,
        out_specs=IN_VMEM,
        out_shape=jax.ShapeDtypeStruct((PAD, w_out.shape[0]), BF16),
        compiler_params=params(16),
        cost_estimate=cost(0.8),
        name="row_sums",
    )(w_out, before)


def bias_kernel(side, n_slabs, n_blocks, ids, window, queries, _, out):
    rows = n_blocks * BLK
    shifted = lax.broadcasted_iota(jnp.int32, (BLK, BLK), 0) - lax.broadcasted_iota(
        jnp.int32, (BLK, BLK), 1
    )
    gaps = {
        by: jnp.abs(shifted + by * BLK).astype(F32) for by in range(1 - n_blocks, n_blocks)
    }
    lane = lax.broadcasted_iota(jnp.int32, (PAD, queries.shape[1]), 1)
    masks = queries[rows : rows + PAD, :].astype(F32)
    query_slab = ids[side]
    for c in range(n_slabs):
        key_slab = ids[4 + c]
        distance = jnp.abs(key_slab - query_slab)
        before = jnp.where(key_slab < query_slab, 0, 1)
        first = jnp.where(distance == 1, before * n_blocks, HD + key_slab * n_blocks)
        whole = jnp.where(distance == 0, 1.0, 0.0)
        reach = window[distance].astype(F32)
        for j in range(n_blocks):
            picked = jnp.sum(jnp.where(lane == first + j, masks, 0.0), axis=1, keepdims=True)
            limit = jnp.where(jnp.maximum(picked, whole) > 0.5, reach, 0.0)
            for i in range(n_blocks):
                here = jnp.broadcast_to(limit[i : i + 1, :], (BLK, BLK))
                out[c, i * BLK : (i + 1) * BLK, j * BLK : (j + 1) * BLK] = jnp.where(
                    gaps[i - j] < here, 0.0, BARRED
                )


def table_kernel(sides, n_slabs, n_blocks, ids, window, _, *tables):
    for side, table in zip(sides, tables):
        lanes, cols = table.shape
        lane = lax.broadcasted_iota(jnp.int32, (lanes, cols), 0)
        col = lax.broadcasted_iota(jnp.int32, (lanes, cols), 1)
        value = jnp.zeros((lanes, cols), F32)
        query_slab = ids[side]
        for c in range(n_slabs):
            key_slab = ids[4 + c]
            distance = jnp.abs(key_slab - query_slab)
            before = jnp.where(key_slab < query_slab, 0, 1)
            first = jnp.where(distance == 1, before * n_blocks, HD + key_slab * n_blocks)
            reach = window[distance].astype(F32)
            here = (lane - first == col - c * n_blocks) & (col // n_blocks == c)
            value = jnp.where(here, reach, value)
        table[...] = value.astype(BF16)


def tables(sides, ids, window, lanes, n_blocks, before):
    n_slabs = ids.shape[0] - 4
    return pl.pallas_call(
        functools.partial(table_kernel, sides, n_slabs, n_blocks),
        in_specs=[IN_SMEM] * 2 + [IN_VMEM],
        out_specs=[IN_VMEM] * len(sides),
        out_shape=[jax.ShapeDtypeStruct((lanes, HD), BF16) for _ in sides],
        compiler_params=params(16),
        cost_estimate=cost(0.5),
        name="tables",
    )(ids, window, before)


def late_bias_kernel(n_slabs, n_blocks, table, queries, _, out):
    rows = n_blocks * BLK
    limits = jnp.dot(queries[rows : rows + PAD, :], table[...], preferred_element_type=F32)
    shifted = lax.broadcasted_iota(jnp.int32, (BLK, BLK), 0) - lax.broadcasted_iota(
        jnp.int32, (BLK, BLK), 1
    )
    gaps = {
        by: jnp.abs(shifted + by * BLK).astype(F32) for by in range(1 - n_blocks, n_blocks)
    }
    for c in range(n_slabs):
        for i in range(n_blocks):
            for j in range(n_blocks):
                at = c * n_blocks + j
                here = jnp.broadcast_to(limits[i : i + 1, at : at + 1], (BLK, BLK))
                out[c, i * BLK : (i + 1) * BLK, j * BLK : (j + 1) * BLK] = jnp.where(
                    gaps[i - j] < here, 0.0, BARRED
                )


def biases(side, ids, window, queries, n_blocks, before):
    n_slabs = ids.shape[0] - 4
    rows = n_blocks * BLK
    return pl.pallas_call(
        functools.partial(bias_kernel, side, n_slabs, n_blocks),
        in_specs=[IN_SMEM] * 2 + [IN_VMEM] * 2,
        out_specs=IN_VMEM,
        out_shape=jax.ShapeDtypeStruct((n_slabs, rows, rows), F32),
        compiler_params=params(16),
        cost_estimate=cost(0.5),
        name="biases",
    )(ids, window, queries, before)


def attend_body(slabs, packed, heads, bias, queries, chunks, before, out):
    rows = bias.shape[1]
    ones = jnp.ones((rows, HD), BF16)
    if packed:
        out[rows:, :] = jnp.zeros((PAD, out.shape[1]), BF16)
    for h in range(*heads):
        span = slice(h * HD, (h + 1) * HD)
        keys = jnp.concatenate([key[:, span] for key, _ in chunks], axis=0)
        scores = lax.dot_general(
            queries[:rows, span], keys, (((1,), (1,)), ((), ())), preferred_element_type=F32
        )
        weights = [
            jnp.exp(scores[:, n * rows : (n + 1) * rows] + bias[slab]).astype(BF16)
            for n, slab in enumerate(slabs)
        ]
        values = jnp.concatenate(
            [jnp.concatenate([value[:, span], ones], axis=1) for _, value in chunks], axis=0
        )
        sums = jnp.dot(jnp.concatenate(weights, axis=1), values, preferred_element_type=F32)
        if before is not None:
            sums = sums + before[h]
        if not packed:
            out[h] = sums
            continue
        span = slice((h - heads[0]) * HD, (h - heads[0] + 1) * HD)
        out[:rows, span] = sums[:, :HD].astype(BF16)
        for b in range(rows // HD):
            pack_denominator(out, rows, b, span, sums[b * HD : (b + 1) * HD, HD:])


def taken_chunks(lone, rows, refs):
    chunks = []
    for apart in lone:
        if apart:
            keys, values = refs.pop(0), refs.pop(0)
            chunks.append((keys.at[:rows], values.at[values.shape[0] - rows :]))
        else:
            both = refs.pop(0)
            chunks.append((both.at[:rows], both.at[rows:]))
    return chunks


def other_kernel(slabs, lone, heads, n_blocks, table, queries, _, *refs):
    refs = list(refs)
    rows = n_blocks * BLK
    chunks = taken_chunks(lone, rows, refs)
    out, bias = refs
    late_bias_kernel(bias.shape[0], n_blocks, table, queries, None, bias)
    attend_body(slabs, False, heads, bias, queries, chunks, None, out)


def attend_other(table, queries, before, parts, n_slabs, n_blocks, heads, name):
    rows = n_blocks * BLK
    operands = [table, queries, before] + [array for chunk, _ in parts for array in chunk]
    return pl.pallas_call(
        functools.partial(
            other_kernel, [s for _, s in parts], [len(c) > 1 for c, _ in parts], heads, n_blocks
        ),
        in_specs=[IN_VMEM] * len(operands),
        out_specs=[IN_VMEM] * 2,
        out_shape=[
            jax.ShapeDtypeStruct((heads[1] - heads[0], rows, 2 * HD), F32),
            jax.ShapeDtypeStruct((n_slabs, rows, rows), F32),
        ],
        compiler_params=params(24),
        cost_estimate=cost(1.0),
        name=name,
    )(*operands)


def attend_kernel(slabs, lone, has_totals, heads, bias, queries, _, *refs):
    refs = list(refs)
    chunks = taken_chunks(lone, bias.shape[1], refs)
    before, out = (refs[0], refs[1]) if has_totals else (None, refs[0])
    attend_body(slabs, False, heads, bias, queries, chunks, before, out)


def pair_kernel(slabs, lone, heads, first_bias, first, second_bias, second, *refs):
    refs = list(refs)
    rows = first_bias.shape[1]
    chunks = taken_chunks(lone, rows, refs)
    first_totals, second_totals, out = refs
    held = rows + PAD
    attend_body(slabs, True, heads, first_bias, first, chunks, first_totals, out.at[:held])
    attend_body(slabs, True, heads, second_bias, second, chunks, second_totals, out.at[held:])


def attend_pair(first, second, parts, heads, name):
    rows = first[0].shape[1]
    operands = [first[0], first[1], second[0], second[1]]
    operands += [array for chunk, _ in parts for array in chunk] + [first[2], second[2]]
    return pl.pallas_call(
        functools.partial(
            pair_kernel, [slab for _, slab in parts], [len(c) > 1 for c, _ in parts], heads
        ),
        in_specs=[IN_VMEM] * len(operands),
        out_specs=IN_VMEM,
        out_shape=jax.ShapeDtypeStruct((2 * (rows + PAD), (heads[1] - heads[0]) * HD), BF16),
        compiler_params=params(24),
        cost_estimate=cost(0.6),
        name=name,
    )(*operands)


def attend(bias, queries, before, parts, totals, heads, name):
    rows = bias.shape[1]
    operands = [bias, queries, before] + [array for chunk, _ in parts for array in chunk]
    if totals is not None:
        operands.append(totals)
    count = heads[1] - heads[0]
    shape = jax.ShapeDtypeStruct((count, rows, 2 * HD), F32)
    slabs = [slab for _, slab in parts]
    return pl.pallas_call(
        functools.partial(
            attend_kernel, slabs, [len(c) > 1 for c, _ in parts], totals is not None, heads
        ),
        in_specs=[IN_VMEM] * len(operands),
        out_specs=IN_VMEM,
        out_shape=shape,
        compiler_params=params(24),
        cost_estimate=cost(0.08 * len(parts) * count + 0.15),
        name=name,
    )(*operands)


def packed_sums(packed, first, rows, block, span):
    here = slice(first + block * HD, first + (block + 1) * HD)
    pair = packed[first + rows : first + rows + PAD, span].astype(F32)
    row = pair[2 * block : 2 * block + 1, :] + pair[2 * block + 1 : 2 * block + 2, :]
    return packed[here, span].astype(F32), jnp.broadcast_to(row, (HD, HD)).T


def pack_denominator(out, rows, block, span, denominator):
    row = denominator.T[0:1, :]
    high = row.astype(BF16)
    out[rows + 2 * block : rows + 2 * block + 1, span] = high
    out[rows + 2 * block + 1 : rows + 2 * block + 2, span] = (row - high.astype(F32)).astype(BF16)


def join_kernel(last, firsts, kept, *refs):
    got, out = refs[:-2], refs[-1]
    heads, rows, _ = kept.shape
    if not last:
        out[rows:, :] = jnp.zeros((PAD, out.shape[1]), BF16)
    for h in range(heads):
        span = slice(h * HD, (h + 1) * HD)
        for b in range(rows // HD):
            here = slice(b * HD, (b + 1) * HD)
            num, den = kept[h, here, :HD], kept[h, here, HD:]
            for first, packed in zip(firsts, got):
                more_num, more_den = packed_sums(packed, first, rows, b, span)
                num, den = num + more_num, den + more_den
            if last:
                out[here, span] = (num / den).astype(BF16)
            else:
                out[here, span] = num.astype(BF16)
                pack_denominator(out, rows, b, span, den)


def join(kept, got, last, before):
    heads, rows, _ = kept.shape
    return pl.pallas_call(
        functools.partial(join_kernel, last, [first for _, first in got]),
        in_specs=[IN_VMEM] * (2 + len(got)),
        out_specs=IN_VMEM,
        out_shape=jax.ShapeDtypeStruct((rows + (0 if last else PAD), heads * HD), BF16),
        compiler_params=params(16),
        cost_estimate=cost(0.15),
        name="finish" if last else "join",
    )(kept, *[array for array, _ in got], before)


def gate_kernel(array, _, out):
    pass


def gate_all_kernel(*refs):
    pass


def gate_all(arrays, before):
    n = len(arrays)
    return pl.pallas_call(
        gate_all_kernel,
        in_specs=[IN_VMEM] * (n + 1),
        out_specs=[IN_VMEM] * n,
        out_shape=[jax.ShapeDtypeStruct(array.shape, array.dtype) for array in arrays],
        input_output_aliases={i: i for i in range(n)},
        compiler_params=params(16),
        cost_estimate=cost(0.1),
        name="gate_all",
    )(*arrays, before)


def copy_kernel(array, _, out):
    out[...] = array[...]


def copied(array, before):
    return pl.pallas_call(
        copy_kernel,
        in_specs=[IN_VMEM] * 2,
        out_specs=IN_VMEM,
        out_shape=jax.ShapeDtypeStruct(array.shape, array.dtype),
        compiler_params=params(16),
        cost_estimate=cost(0.1),
        name="copied",
    )(array, before)


def gate(array, before):
    return pl.pallas_call(
        gate_kernel,
        in_specs=[IN_VMEM] * 2,
        out_specs=IN_VMEM,
        out_shape=jax.ShapeDtypeStruct(array.shape, array.dtype),
        input_output_aliases={0: 0},
        compiler_params=params(16),
        cost_estimate=cost(0.1),
        name="gate",
    )(array, before)


def row_dot(summed, values):
    dots = lax.dot_general(
        summed, values, (((1,), (1,)), ((), ())), preferred_element_type=F32
    )
    return dots[0:1, :] + (dots[1:2, :] + dots[2:3, :])


def early_kernel(n_head, place, own, w_out, sums, received, partial, parts, owners, held):
    cols = partial.shape[1]
    first = pl.multiple_of(place[0] * cols, HD)
    partial[...] = jnp.dot(own[...], w_out[:, pl.ds(first, cols)], preferred_element_type=F32)
    held[...] = received[...]
    parts[...] = jnp.zeros(parts.shape, F32)
    parts[pl.ds(place[0], 1), :] = row_dot(sums[...], own[...])
    row = lax.broadcasted_iota(jnp.int32, parts.shape, 0)
    for k in range(1, n_head):
        owner = lax.rem(place[0] - k + n_head, n_head)
        owners[k - 1] = jnp.where(row == owner, 1.0, 0.0)


def project_early(place, own, w_out, sums, received, n_head):
    rows = own.shape[0]
    cols = w_out.shape[1] // n_head
    places = -(-n_head // 8) * 8
    return pl.pallas_call(
        functools.partial(early_kernel, n_head),
        in_specs=[IN_SMEM] + [IN_VMEM] * 4,
        out_specs=[IN_VMEM] * 4,
        out_shape=[
            jax.ShapeDtypeStruct((rows, cols), F32),
            jax.ShapeDtypeStruct((places, rows), F32),
            jax.ShapeDtypeStruct((n_head - 1, places, rows), F32),
            jax.ShapeDtypeStruct(received.shape, BF16),
        ],
        compiler_params=params(24),
        cost_estimate=cost(1.4),
        name="project_early",
    )(place, own, w_out, sums, received)


def last_kernel(n_head, *refs):
    late, refs = refs[: n_head - 1], refs[n_head - 1 :]
    received, sums, partial, parts, owners, layer_out, checksum, staged, summed, sems = refs
    rows, cols = partial.shape
    tiles = sems.shape[0] - 1
    tile = cols // tiles
    stores = []
    for t in range(tiles):
        here = slice(t * tile, (t + 1) * tile)
        total = partial[:, here]
        for k in range(1, n_head):
            total = total + jnp.dot(
                late[k - 1][...], received[k - 1, :, here], preferred_element_type=F32
            )
        staged[:, here] = total.astype(BF16)
        there = pl.ds(t * tile, tile)
        stores.append(
            pltpu.make_async_copy(staged.at[:, there], layer_out.at[:, there], sems.at[t])
        )
        stores[-1].start()
        if t > 0:
            continue
        every = parts[...]
        for k in range(1, n_head):
            dot = row_dot(sums[(k - 1) * PAD : k * PAD, :], late[k - 1][...])
            every = every + owners[k - 1] * dot
        sum_all = every[0:1, :]
        for k in range(1, n_head):
            sum_all = sum_all + every[k : k + 1, :]
        summed[...] = sum_all * D ** (-0.5)
        stores.append(pltpu.make_async_copy(summed, checksum, sems.at[tiles]))
        stores[-1].start()
    for store in stores:
        store.wait()


def project_last(late, received, sums, partial, parts, owners):
    n_head = len(late) + 1
    rows, cols = partial.shape
    tiles = next(t for t in (3, 2, 1) if cols % (t * HD) == 0)
    operands = [*late, received, sums, partial, parts, owners]
    layer_out, checksum = pl.pallas_call(
        functools.partial(last_kernel, n_head),
        in_specs=[IN_VMEM] * len(operands),
        out_specs=[ANYWHERE] * 2,
        out_shape=[
            jax.ShapeDtypeStruct((rows, cols), BF16),
            jax.ShapeDtypeStruct((1, rows), F32),
        ],
        scratch_shapes=[
            VMEM((rows, cols), BF16),
            VMEM((1, rows), F32),
            pltpu.SemaphoreType.DMA((tiles + 1,)),
        ],
        compiler_params=params(24),
        name="project_last",
    )(*operands)
    return layer_out, checksum.reshape(rows)


def per_device(tokens, w_qkv, norm_gains, w_out, near_mask, far_pattern, window):
    rows = tokens.shape[0]
    heads = w_qkv.shape[2] // HD
    n_blocks = rows // BLK
    frame = lax.axis_index("frame").astype(jnp.int32)
    place = lax.axis_index("head").astype(jnp.int32).reshape(1)
    n_frame = lax.axis_size("frame")
    n_head = lax.axis_size("head")
    half = n_frame // 2
    every = (0, heads)

    def swapped(array, by):
        return lax.ppermute(array, "frame", [(i, i ^ by) for i in range(n_frame)])

    def from_head(array, k):
        return lax.ppermute(array, "head", [(i, (i + k) % n_head) for i in range(n_head)])

    def from_heads(arrays):
        got = [from_head(array, k) for k, array in enumerate(arrays, 1)]
        return got[0] if len(got) == 1 else jnp.concatenate(got)

    spans = []
    by = half // 2
    while by > 1:
        spans.append(by)
        by //= 2
    far = sorted((o for o in range(2, half, 2) if o not in spans), key=lambda o: bin(o).count("1"))
    slabs = [0] + spans + far
    n_near = 1 + len(spans)

    kv, queries = project(tokens, w_qkv, norm_gains, near_mask, far_pattern)
    near = {by: swapped(kv, by) for by in spans}
    sib_queries = swapped(queries, 1)
    ids = jnp.stack([frame ^ o for o in [0, 1, half, half ^ 1] + slabs])

    def bias_of(side, array, before):
        return biases(side, ids, window, array, n_blocks, before)

    mine = [((kv,), 0)]
    own_bias = bias_of(0, queries, queries)
    own = attend(own_bias, queries, own_bias, mine, None, every, "attend_first")
    other_queries = swapped(copied(queries, own), half)
    payload = columns_of(w_out, n_head, own)
    received = from_heads([payload[k - 1 : k] for k in range(1, n_head)])
    other_table, other_sib_table = tables(
        (2, 3), ids, window, queries.shape[1], n_blocks, own
    )
    sib_bias = bias_of(1, sib_queries, other_sib_table)
    sib = attend(sib_bias, sib_queries, sib_bias, mine, None, every, "sibling_first")

    near = dict(zip(spans, gate_all([near[by] for by in spans], sib)))
    keys = {by: near[by][: rows + 2 * PAD] for by in spans}
    values = {by: near[by][rows - 3 * PAD :] for by in spans}
    for o in far:
        bits = [by for by in spans if o & by]
        values[o] = swapped(values[o ^ bits[0]], bits[0])
        keys[o] = swapped(keys[o ^ bits[-1]], bits[-1])
    early = [((near[by],), i) for i, by in enumerate(spans, 1)]
    sib = attend(sib_bias, sib_queries, sib_bias, early, sib, every, "sibling_second")
    own = attend(own_bias, queries, sib, early, own, every, "attend_second")
    other_queries = gate(other_queries, own)
    other_sib = swapped(other_queries, 1)
    other, other_bias = attend_other(
        other_table, other_queries, own, mine + early, len(slabs), n_blocks, every, "other_first"
    )
    both, other_sib_bias = attend_other(
        other_sib_table, other_sib, other, mine + early, len(slabs), n_blocks, every, "other_sibling_first"
    )
    late = []
    for i, o in enumerate(far, n_near):
        late.append(((gate(keys[o], both), gate(values[o], both)), i))
    across = attend_pair(
        (other_sib_bias, other_sib, both), (sib_bias, sib_queries, sib), late, every, "attend_pair"
    )
    other = attend(other_bias, other_queries, across, late, other, every, "other_last")
    own = attend(own_bias, queries, other, late, own, every, "attend_last")
    from_core = swapped(across, 1)
    sent = join(other, [(from_core, 0)], False, own)
    got = swapped(sent, half)
    sums = row_sums(w_out, sent)
    done = join(own, [(from_core, rows + PAD), (got, 0)], True, sums)
    other_sums = from_heads([sums] * (n_head - 1))
    late = [from_head(done, k) for k in range(1, n_head)]
    partial, sum_parts, owners, received = project_early(
        place, done, w_out, sums, received, n_head
    )
    return project_last(late, received, other_sums, partial, sum_parts, owners)


def solution(mesh):
    in_specs = (
        P("frame", None),
        P(None, None, "head"),
        P(None, "head"),
        P("head", None),
        P("frame", None),
        P("frame", None),
        P(),
    )
    out_specs = (P("frame", "head"), P("frame"))
    return jax.shard_map(
        per_device, mesh=mesh, in_specs=in_specs, out_specs=out_specs, check_vma=False
    )
```

```python
import functools

import jax
import jax.numpy as jnp
from jax import lax
from jax.experimental import pallas as pl
from jax.experimental.pallas import tpu as pltpu
from jax.sharding import PartitionSpec as P

D = 3072
HD = 128
BLK = 128
EPS = 1e-06
PAD = 16
BARRED = -1e30
F32 = jnp.float32
BF16 = jnp.bfloat16
VMEM = pltpu.VMEM
SMEM = pltpu.SMEM
MIB = 1024 * 1024
IN_VMEM = pl.BlockSpec(memory_space=VMEM)
IN_SMEM = pl.BlockSpec(memory_space=SMEM)
IN_HBM = pl.BlockSpec(memory_space=pltpu.HBM)
ANYWHERE = pl.BlockSpec(memory_space=pl.ANY)


def params(mib):
    return pltpu.CompilerParams(vmem_limit_bytes=mib * MIB)


def cost(microseconds):
    return pl.CostEstimate(
        flops=int(microseconds * 0), bytes_accessed=int(microseconds * 0), transcendentals=0
    )


def normed(values, gains, scale):
    parts = []
    for first in range(0, values.shape[1], HD):
        head = values[:, first : first + HD]
        factor = lax.rsqrt(jnp.mean(head * head, axis=-1, keepdims=True) + EPS)
        parts.append(head * factor * gains[:, first : first + HD] * scale)
    return jnp.concatenate(parts, axis=1)


def project_kernel(steps, tokens, w_qkv, gains, near_mask, far_pattern, kv, queries, *scratch):
    token_buf, w_buf, gain_buf, near_buf, far_buf, total, sems, small_sems = scratch
    rows, width = tokens.shape
    count, _, cols = w_qkv.shape
    deep = width // steps
    copies = []
    for s in range(steps):
        span = pl.ds(s * deep, deep)
        group = [pltpu.make_async_copy(tokens.at[:, span], token_buf.at[:, span], sems.at[0, s])]
        for j in range(count):
            group.append(
                pltpu.make_async_copy(
                    w_qkv.at[j, span], w_buf.at[span, pl.ds(j * cols, cols)], sems.at[1 + j, s]
                )
            )
        for copy in group:
            copy.start()
        copies.append(group)
    small = [
        pltpu.make_async_copy(source, target, small_sems.at[i])
        for i, (source, target) in enumerate(
            ((gains, gain_buf), (near_mask, near_buf), (far_pattern, far_buf))
        )
    ]
    for copy in small:
        copy.start()
    for s in range(steps):
        for copy in copies[s]:
            copy.wait()
        span = slice(s * deep, (s + 1) * deep)
        part = jnp.dot(token_buf[:, span], w_buf[span, :], preferred_element_type=F32)
        if s == 0:
            total[...] = part
        elif s < steps - 1:
            total[...] += part
    part = total[...] + part
    for copy in small:
        copy.wait()
    query, key, value = (part[:, j * cols : (j + 1) * cols] for j in range(count))
    kv[:rows, :] = normed(key, gain_buf[1:2, :], 1.0).astype(BF16)
    kv[rows:, :] = value.astype(BF16)
    queries[:rows, :] = normed(query, gain_buf[0:1, :], HD ** (-0.5)).astype(BF16)
    n_blocks, n_near = near_mask.shape
    queries[rows:, :] = jnp.zeros((PAD, cols), BF16)
    queries[rows : rows + n_blocks, :n_near] = near_buf[...].astype(F32).astype(BF16)
    queries[rows : rows + n_blocks, HD : HD + far_pattern.shape[1]] = (
        far_buf[...].astype(F32).astype(BF16)
    )


def project(tokens, w_qkv, gains, near_mask, far_pattern):
    rows, width = tokens.shape
    count, _, cols = w_qkv.shape
    steps = 4
    return pl.pallas_call(
        functools.partial(project_kernel, steps),
        in_specs=[ANYWHERE] * 5,
        out_specs=[IN_VMEM] * 2,
        out_shape=[
            jax.ShapeDtypeStruct((2 * rows, cols), BF16),
            jax.ShapeDtypeStruct((rows + PAD, cols), BF16),
        ],
        scratch_shapes=[
            VMEM((rows, width), BF16),
            VMEM((width, count * cols), BF16),
            VMEM(gains.shape, F32),
            VMEM(near_mask.shape, jnp.int32),
            VMEM(far_pattern.shape, jnp.int32),
            VMEM((rows, count * cols), F32),
            pltpu.SemaphoreType.DMA((1 + count, steps)),
            pltpu.SemaphoreType.DMA((3,)),
        ],
        compiler_params=params(56),
        cost_estimate=cost(5.0),
        name="project",
    )(tokens, w_qkv, gains, near_mask, far_pattern)


def split_sum(values):
    high = values.astype(BF16).astype(F32)
    mid = (values - high).astype(BF16).astype(F32)
    return high, mid, values - high - mid


def columns_kernel(n_head, w_out, _, payload, sems):
    cols = payload.shape[2]
    place = lax.axis_index("head")
    copies = []
    for k in range(1, n_head):
        first = pl.multiple_of(lax.rem(place + k, n_head) * cols, HD)
        copies.append(
            pltpu.make_async_copy(w_out.at[:, pl.ds(first, cols)], payload.at[k - 1], sems.at[k - 1])
        )
    for copy in copies:
        copy.start()
    for copy in copies:
        copy.wait()


def columns_of(w_out, n_head, before):
    rows, width = w_out.shape
    return pl.pallas_call(
        functools.partial(columns_kernel, n_head),
        in_specs=[ANYWHERE, IN_VMEM],
        out_specs=IN_VMEM,
        out_shape=jax.ShapeDtypeStruct((n_head - 1, rows, width // n_head), BF16),
        scratch_shapes=[pltpu.SemaphoreType.DMA((n_head - 1,))],
        compiler_params=params(16),
        cost_estimate=cost(1.0),
        name="columns",
    )(w_out, before)


def sums_kernel(w_out, _, sums):
    rows, width = w_out.shape
    total = lax.dot_general(
        jnp.ones((8, width), BF16), w_out[...], (((1,), (1,)), ((), ())), preferred_element_type=F32
    )
    high, mid, low = split_sum(total)
    row = lax.broadcasted_iota(jnp.int32, (8, rows), 0)
    packed = jnp.where(row == 0, high, jnp.where(row == 1, mid, jnp.where(row == 2, low, 0.0)))
    sums[...] = jnp.concatenate([packed, jnp.zeros((PAD - 8, rows), F32)], axis=0).astype(BF16)


def row_sums(w_out, before):
    return pl.pallas_call(
        sums_kernel,
        in_specs=[IN_VMEM] * 2,
        out_specs=IN_VMEM,
        out_shape=jax.ShapeDtypeStruct((PAD, w_out.shape[0]), BF16),
        compiler_params=params(16),
        cost_estimate=cost(0.8),
        name="row_sums",
    )(w_out, before)


def bias_kernel(side, n_slabs, n_blocks, ids, window, queries, _, out):
    rows = n_blocks * BLK
    shifted = lax.broadcasted_iota(jnp.int32, (BLK, BLK), 0) - lax.broadcasted_iota(
        jnp.int32, (BLK, BLK), 1
    )
    gaps = {
        by: jnp.abs(shifted + by * BLK).astype(F32) for by in range(1 - n_blocks, n_blocks)
    }
    lane = lax.broadcasted_iota(jnp.int32, (PAD, queries.shape[1]), 1)
    masks = queries[rows : rows + PAD, :].astype(F32)
    query_slab = ids[side]
    for c in range(n_slabs):
        key_slab = ids[4 + c]
        distance = jnp.abs(key_slab - query_slab)
        before = jnp.where(key_slab < query_slab, 0, 1)
        first = jnp.where(distance == 1, before * n_blocks, HD + key_slab * n_blocks)
        whole = jnp.where(distance == 0, 1.0, 0.0)
        reach = window[distance].astype(F32)
        for j in range(n_blocks):
            picked = jnp.sum(jnp.where(lane == first + j, masks, 0.0), axis=1, keepdims=True)
            limit = jnp.where(jnp.maximum(picked, whole) > 0.5, reach, 0.0)
            for i in range(n_blocks):
                here = jnp.broadcast_to(limit[i : i + 1, :], (BLK, BLK))
                out[c, i * BLK : (i + 1) * BLK, j * BLK : (j + 1) * BLK] = jnp.where(
                    gaps[i - j] < here, 0.0, BARRED
                )


def table_kernel(sides, n_slabs, n_blocks, ids, window, _, *tables):
    for side, table in zip(sides, tables):
        lanes, cols = table.shape
        lane = lax.broadcasted_iota(jnp.int32, (lanes, cols), 0)
        col = lax.broadcasted_iota(jnp.int32, (lanes, cols), 1)
        value = jnp.zeros((lanes, cols), F32)
        query_slab = ids[side]
        for c in range(n_slabs):
            key_slab = ids[4 + c]
            distance = jnp.abs(key_slab - query_slab)
            before = jnp.where(key_slab < query_slab, 0, 1)
            first = jnp.where(distance == 1, before * n_blocks, HD + key_slab * n_blocks)
            reach = window[distance].astype(F32)
            here = (lane - first == col - c * n_blocks) & (col // n_blocks == c)
            value = jnp.where(here, reach, value)
        table[...] = value.astype(BF16)


def tables(sides, ids, window, lanes, n_blocks, before):
    n_slabs = ids.shape[0] - 4
    return pl.pallas_call(
        functools.partial(table_kernel, sides, n_slabs, n_blocks),
        in_specs=[IN_SMEM] * 2 + [IN_VMEM],
        out_specs=[IN_VMEM] * len(sides),
        out_shape=[jax.ShapeDtypeStruct((lanes, HD), BF16) for _ in sides],
        compiler_params=params(16),
        cost_estimate=cost(0.5),
        name="tables",
    )(ids, window, before)


def late_bias_kernel(n_slabs, n_blocks, table, queries, _, out):
    rows = n_blocks * BLK
    limits = jnp.dot(queries[rows : rows + PAD, :], table[...], preferred_element_type=F32)
    shifted = lax.broadcasted_iota(jnp.int32, (BLK, BLK), 0) - lax.broadcasted_iota(
        jnp.int32, (BLK, BLK), 1
    )
    gaps = {
        by: jnp.abs(shifted + by * BLK).astype(F32) for by in range(1 - n_blocks, n_blocks)
    }
    for c in range(n_slabs):
        for i in range(n_blocks):
            for j in range(n_blocks):
                at = c * n_blocks + j
                here = jnp.broadcast_to(limits[i : i + 1, at : at + 1], (BLK, BLK))
                out[c, i * BLK : (i + 1) * BLK, j * BLK : (j + 1) * BLK] = jnp.where(
                    gaps[i - j] < here, 0.0, BARRED
                )


def biases(side, ids, window, queries, n_blocks, before):
    n_slabs = ids.shape[0] - 4
    rows = n_blocks * BLK
    return pl.pallas_call(
        functools.partial(bias_kernel, side, n_slabs, n_blocks),
        in_specs=[IN_SMEM] * 2 + [IN_VMEM] * 2,
        out_specs=IN_VMEM,
        out_shape=jax.ShapeDtypeStruct((n_slabs, rows, rows), F32),
        compiler_params=params(16),
        cost_estimate=cost(0.5),
        name="biases",
    )(ids, window, queries, before)


def attend_body(slabs, packed, heads, bias, queries, chunks, before, out):
    rows = bias.shape[1]
    ones = jnp.ones((rows, HD), BF16)
    if packed:
        out[rows:, :] = jnp.zeros((PAD, out.shape[1]), BF16)
    for h in range(*heads):
        span = slice(h * HD, (h + 1) * HD)
        keys = jnp.concatenate([key[:, span] for key, _ in chunks], axis=0)
        scores = lax.dot_general(
            queries[:rows, span], keys, (((1,), (1,)), ((), ())), preferred_element_type=F32
        )
        weights = [
            jnp.exp(scores[:, n * rows : (n + 1) * rows] + bias[slab]).astype(BF16)
            for n, slab in enumerate(slabs)
        ]
        values = jnp.concatenate(
            [jnp.concatenate([value[:, span], ones], axis=1) for _, value in chunks], axis=0
        )
        sums = jnp.dot(jnp.concatenate(weights, axis=1), values, preferred_element_type=F32)
        if before is not None:
            sums = sums + before[h]
        if not packed:
            out[h] = sums
            continue
        span = slice((h - heads[0]) * HD, (h - heads[0] + 1) * HD)
        out[:rows, span] = sums[:, :HD].astype(BF16)
        for b in range(rows // HD):
            pack_denominator(out, rows, b, span, sums[b * HD : (b + 1) * HD, HD:])


def taken_chunks(lone, rows, refs):
    chunks = []
    for apart in lone:
        if apart:
            keys, values = refs.pop(0), refs.pop(0)
            chunks.append((keys.at[:rows], values.at[values.shape[0] - rows :]))
        else:
            both = refs.pop(0)
            chunks.append((both.at[:rows], both.at[rows:]))
    return chunks


def other_kernel(slabs, lone, heads, n_blocks, table, queries, _, *refs):
    refs = list(refs)
    rows = n_blocks * BLK
    chunks = taken_chunks(lone, rows, refs)
    out, bias = refs
    late_bias_kernel(bias.shape[0], n_blocks, table, queries, None, bias)
    attend_body(slabs, False, heads, bias, queries, chunks, None, out)


def attend_other(table, queries, before, parts, n_slabs, n_blocks, heads, name):
    rows = n_blocks * BLK
    operands = [table, queries, before] + [array for chunk, _ in parts for array in chunk]
    return pl.pallas_call(
        functools.partial(
            other_kernel, [s for _, s in parts], [len(c) > 1 for c, _ in parts], heads, n_blocks
        ),
        in_specs=[IN_VMEM] * len(operands),
        out_specs=[IN_VMEM] * 2,
        out_shape=[
            jax.ShapeDtypeStruct((heads[1] - heads[0], rows, 2 * HD), F32),
            jax.ShapeDtypeStruct((n_slabs, rows, rows), F32),
        ],
        compiler_params=params(24),
        cost_estimate=cost(1.0),
        name=name,
    )(*operands)


def attend_kernel(slabs, lone, has_totals, heads, bias, queries, _, *refs):
    refs = list(refs)
    chunks = taken_chunks(lone, bias.shape[1], refs)
    before, out = (refs[0], refs[1]) if has_totals else (None, refs[0])
    attend_body(slabs, False, heads, bias, queries, chunks, before, out)


def pair_kernel(slabs, lone, heads, first_bias, first, second_bias, second, *refs):
    refs = list(refs)
    rows = first_bias.shape[1]
    chunks = taken_chunks(lone, rows, refs)
    first_totals, second_totals, out = refs
    held = rows + PAD
    attend_body(slabs, True, heads, first_bias, first, chunks, first_totals, out.at[:held])
    attend_body(slabs, True, heads, second_bias, second, chunks, second_totals, out.at[held:])


def attend_pair(first, second, parts, heads, name):
    rows = first[0].shape[1]
    operands = [first[0], first[1], second[0], second[1]]
    operands += [array for chunk, _ in parts for array in chunk] + [first[2], second[2]]
    return pl.pallas_call(
        functools.partial(
            pair_kernel, [slab for _, slab in parts], [len(c) > 1 for c, _ in parts], heads
        ),
        in_specs=[IN_VMEM] * len(operands),
        out_specs=IN_VMEM,
        out_shape=jax.ShapeDtypeStruct((2 * (rows + PAD), (heads[1] - heads[0]) * HD), BF16),
        compiler_params=params(24),
        cost_estimate=cost(0.6),
        name=name,
    )(*operands)


def attend(bias, queries, before, parts, totals, heads, name):
    rows = bias.shape[1]
    operands = [bias, queries, before] + [array for chunk, _ in parts for array in chunk]
    if totals is not None:
        operands.append(totals)
    count = heads[1] - heads[0]
    shape = jax.ShapeDtypeStruct((count, rows, 2 * HD), F32)
    slabs = [slab for _, slab in parts]
    return pl.pallas_call(
        functools.partial(
            attend_kernel, slabs, [len(c) > 1 for c, _ in parts], totals is not None, heads
        ),
        in_specs=[IN_VMEM] * len(operands),
        out_specs=IN_VMEM,
        out_shape=shape,
        compiler_params=params(24),
        cost_estimate=cost(0.08 * len(parts) * count + 0.15),
        name=name,
    )(*operands)


def packed_sums(packed, first, rows, block, span):
    here = slice(first + block * HD, first + (block + 1) * HD)
    pair = packed[first + rows : first + rows + PAD, span].astype(F32)
    row = pair[2 * block : 2 * block + 1, :] + pair[2 * block + 1 : 2 * block + 2, :]
    return packed[here, span].astype(F32), jnp.broadcast_to(row, (HD, HD)).T


def pack_denominator(out, rows, block, span, denominator):
    row = denominator.T[0:1, :]
    high = row.astype(BF16)
    out[rows + 2 * block : rows + 2 * block + 1, span] = high
    out[rows + 2 * block + 1 : rows + 2 * block + 2, span] = (row - high.astype(F32)).astype(BF16)


def join_kernel(last, firsts, kept, *refs):
    got, out = refs[:-2], refs[-1]
    heads, rows, _ = kept.shape
    if not last:
        out[rows:, :] = jnp.zeros((PAD, out.shape[1]), BF16)
    for h in range(heads):
        span = slice(h * HD, (h + 1) * HD)
        for b in range(rows // HD):
            here = slice(b * HD, (b + 1) * HD)
            num, den = kept[h, here, :HD], kept[h, here, HD:]
            for first, packed in zip(firsts, got):
                more_num, more_den = packed_sums(packed, first, rows, b, span)
                num, den = num + more_num, den + more_den
            if last:
                out[here, span] = (num / den).astype(BF16)
            else:
                out[here, span] = num.astype(BF16)
                pack_denominator(out, rows, b, span, den)


def join(kept, got, last, before):
    heads, rows, _ = kept.shape
    return pl.pallas_call(
        functools.partial(join_kernel, last, [first for _, first in got]),
        in_specs=[IN_VMEM] * (2 + len(got)),
        out_specs=IN_VMEM,
        out_shape=jax.ShapeDtypeStruct((rows + (0 if last else PAD), heads * HD), BF16),
        compiler_params=params(16),
        cost_estimate=cost(0.15),
        name="finish" if last else "join",
    )(kept, *[array for array, _ in got], before)


def gate_kernel(array, _, out):
    out[...] = array[...]


def gate_all_kernel(*refs):
    n = len(refs) // 2
    for array, out in zip(refs[:n], refs[n + 1 :]):
        out[...] = array[...]


def gate_all(arrays, before):
    n = len(arrays)
    return pl.pallas_call(
        gate_all_kernel,
        in_specs=[IN_VMEM] * (n + 1),
        out_specs=[IN_VMEM] * n,
        out_shape=[jax.ShapeDtypeStruct(array.shape, array.dtype) for array in arrays],
        input_output_aliases={i: i for i in range(n)},
        compiler_params=params(16),
        cost_estimate=cost(0.1),
        name="gate_all",
    )(*arrays, before)


def copy_kernel(array, _, out):
    out[...] = array[...]


def copied(array, before):
    return pl.pallas_call(
        copy_kernel,
        in_specs=[IN_VMEM] * 2,
        out_specs=IN_VMEM,
        out_shape=jax.ShapeDtypeStruct(array.shape, array.dtype),
        compiler_params=params(16),
        cost_estimate=cost(0.1),
        name="copied",
    )(array, before)


def gate(array, before):
    return pl.pallas_call(
        gate_kernel,
        in_specs=[IN_VMEM] * 2,
        out_specs=IN_VMEM,
        out_shape=jax.ShapeDtypeStruct(array.shape, array.dtype),
        input_output_aliases={0: 0},
        compiler_params=params(16),
        cost_estimate=cost(0.1),
        name="gate",
    )(array, before)


def row_dot(summed, values):
    dots = lax.dot_general(
        summed, values, (((1,), (1,)), ((), ())), preferred_element_type=F32
    )
    return dots[0:1, :] + (dots[1:2, :] + dots[2:3, :])


def early_kernel(n_head, place, own, w_out, sums, received, partial, parts, owners, held):
    cols = partial.shape[1]
    first = pl.multiple_of(place[0] * cols, HD)
    partial[...] = jnp.dot(own[...], w_out[:, pl.ds(first, cols)], preferred_element_type=F32)
    held[...] = received[...]
    parts[...] = jnp.zeros(parts.shape, F32)
    parts[pl.ds(place[0], 1), :] = row_dot(sums[...], own[...])
    row = lax.broadcasted_iota(jnp.int32, parts.shape, 0)
    for k in range(1, n_head):
        owner = lax.rem(place[0] - k + n_head, n_head)
        owners[k - 1] = jnp.where(row == owner, 1.0, 0.0)


def project_early(place, own, w_out, sums, received, n_head):
    rows = own.shape[0]
    cols = w_out.shape[1] // n_head
    places = -(-n_head // 8) * 8
    return pl.pallas_call(
        functools.partial(early_kernel, n_head),
        in_specs=[IN_SMEM] + [IN_VMEM] * 4,
        out_specs=[IN_VMEM] * 4,
        out_shape=[
            jax.ShapeDtypeStruct((rows, cols), F32),
            jax.ShapeDtypeStruct((places, rows), F32),
            jax.ShapeDtypeStruct((n_head - 1, places, rows), F32),
            jax.ShapeDtypeStruct(received.shape, BF16),
        ],
        compiler_params=params(24),
        cost_estimate=cost(1.4),
        name="project_early",
    )(place, own, w_out, sums, received)


def last_kernel(n_head, *refs):
    late, refs = refs[: n_head - 1], refs[n_head - 1 :]
    received, sums, partial, parts, owners, layer_out, checksum, staged, summed, sems = refs
    rows, cols = partial.shape
    tiles = sems.shape[0] - 1
    tile = cols // tiles
    stores = []
    for t in range(tiles):
        here = slice(t * tile, (t + 1) * tile)
        total = partial[:, here]
        for k in range(1, n_head):
            total = total + jnp.dot(
                late[k - 1][...], received[k - 1, :, here], preferred_element_type=F32
            )
        staged[:, here] = total.astype(BF16)
        there = pl.ds(t * tile, tile)
        stores.append(
            pltpu.make_async_copy(staged.at[:, there], layer_out.at[:, there], sems.at[t])
        )
        stores[-1].start()
        if t > 0:
            continue
        every = parts[...]
        for k in range(1, n_head):
            dot = row_dot(sums[(k - 1) * PAD : k * PAD, :], late[k - 1][...])
            every = every + owners[k - 1] * dot
        sum_all = every[0:1, :]
        for k in range(1, n_head):
            sum_all = sum_all + every[k : k + 1, :]
        summed[...] = sum_all * D ** (-0.5)
        stores.append(pltpu.make_async_copy(summed, checksum, sems.at[tiles]))
        stores[-1].start()
    for store in stores:
        store.wait()


def project_last(late, received, sums, partial, parts, owners):
    n_head = len(late) + 1
    rows, cols = partial.shape
    tiles = next(t for t in (3, 2, 1) if cols % (t * HD) == 0)
    operands = [*late, received, sums, partial, parts, owners]
    layer_out, checksum = pl.pallas_call(
        functools.partial(last_kernel, n_head),
        in_specs=[IN_VMEM] * len(operands),
        out_specs=[ANYWHERE] * 2,
        out_shape=[
            jax.ShapeDtypeStruct((rows, cols), BF16),
            jax.ShapeDtypeStruct((1, rows), F32),
        ],
        scratch_shapes=[
            VMEM((rows, cols), BF16),
            VMEM((1, rows), F32),
            pltpu.SemaphoreType.DMA((tiles + 1,)),
        ],
        compiler_params=params(24),
        name="project_last",
    )(*operands)
    return layer_out, checksum.reshape(rows)


def per_device(tokens, w_qkv, norm_gains, w_out, near_mask, far_pattern, window):
    rows = tokens.shape[0]
    heads = w_qkv.shape[2] // HD
    n_blocks = rows // BLK
    frame = lax.axis_index("frame").astype(jnp.int32)
    place = lax.axis_index("head").astype(jnp.int32).reshape(1)
    n_frame = lax.axis_size("frame")
    n_head = lax.axis_size("head")
    half = n_frame // 2
    every = (0, heads)

    def swapped(array, by):
        return lax.ppermute(array, "frame", [(i, i ^ by) for i in range(n_frame)])

    def from_head(array, k):
        return lax.ppermute(array, "head", [(i, (i + k) % n_head) for i in range(n_head)])

    def from_heads(arrays):
        got = [from_head(array, k) for k, array in enumerate(arrays, 1)]
        return got[0] if len(got) == 1 else jnp.concatenate(got)

    spans = []
    by = half // 2
    while by > 1:
        spans.append(by)
        by //= 2
    far = sorted((o for o in range(2, half, 2) if o not in spans), key=lambda o: bin(o).count("1"))
    slabs = [0] + spans + far
    n_near = 1 + len(spans)

    kv, queries = project(tokens, w_qkv, norm_gains, near_mask, far_pattern)
    near = {by: swapped(kv, by) for by in spans}
    sib_queries = swapped(queries, 1)
    ids = jnp.stack([frame ^ o for o in [0, 1, half, half ^ 1] + slabs])

    def bias_of(side, array, before):
        return biases(side, ids, window, array, n_blocks, before)

    mine = [((kv,), 0)]
    own_bias = bias_of(0, queries, queries)
    own = attend(own_bias, queries, own_bias, mine, None, every, "attend_first")
    other_queries = swapped(copied(queries, own), half)
    payload = columns_of(w_out, n_head, own)
    received = from_heads([payload[k - 1 : k] for k in range(1, n_head)])
    other_table, other_sib_table = tables(
        (2, 3), ids, window, queries.shape[1], n_blocks, own
    )
    sib_bias = bias_of(1, sib_queries, other_sib_table)
    sib = attend(sib_bias, sib_queries, sib_bias, mine, None, every, "sibling_first")

    near = dict(zip(spans, gate_all([near[by] for by in spans], sib)))
    keys = {by: near[by][: rows + 2 * PAD] for by in spans}
    values = {by: near[by][rows - 3 * PAD :] for by in spans}
    for o in far:
        bits = [by for by in spans if o & by]
        values[o] = swapped(values[o ^ bits[0]], bits[0])
        keys[o] = swapped(keys[o ^ bits[-1]], bits[-1])
    early = [((near[by],), i) for i, by in enumerate(spans, 1)]
    sib = attend(sib_bias, sib_queries, sib_bias, early, sib, every, "sibling_second")
    own = attend(own_bias, queries, sib, early, own, every, "attend_second")
    other_queries = gate(other_queries, own)
    other_sib = swapped(other_queries, 1)
    other, other_bias = attend_other(
        other_table, other_queries, own, mine + early, len(slabs), n_blocks, every, "other_first"
    )
    both, other_sib_bias = attend_other(
        other_sib_table, other_sib, other, mine + early, len(slabs), n_blocks, every, "other_sibling_first"
    )
    late = []
    for i, o in enumerate(far, n_near):
        late.append(((keys[o], values[o]), i))
    across = attend_pair(
        (other_sib_bias, other_sib, both), (sib_bias, sib_queries, sib), late, every, "attend_pair"
    )
    other = attend(other_bias, other_queries, across, late, other, every, "other_last")
    own = attend(own_bias, queries, other, late, own, every, "attend_last")
    from_core = swapped(across, 1)
    sent = join(other, [(from_core, 0)], False, own)
    got = swapped(sent, half)
    sums = row_sums(w_out, sent)
    done = join(own, [(from_core, rows + PAD), (got, 0)], True, sums)
    other_sums = from_heads([sums] * (n_head - 1))
    late = [from_head(done, k) for k in range(1, n_head)]
    partial, sum_parts, owners, received = project_early(
        place, done, w_out, sums, received, n_head
    )
    return project_last(late, received, other_sums, partial, sum_parts, owners)


def solution(mesh):
    in_specs = (
        P("frame", None),
        P(None, None, "head"),
        P(None, "head"),
        P("head", None),
        P("frame", None),
        P("frame", None),
        P(),
    )
    out_specs = (P("frame", "head"), P("frame"))
    return jax.shard_map(
        per_device, mesh=mesh, in_specs=in_specs, out_specs=out_specs, check_vma=False
    )
```

```python
import functools

import jax
import jax.numpy as jnp
from jax import lax
from jax.experimental import pallas as pl
from jax.experimental.pallas import tpu as pltpu
from jax.sharding import PartitionSpec as P

D = 3072
HD = 128
BLK = 128
EPS = 1e-06
PAD = 16
BARRED = -1e30
F32 = jnp.float32
BF16 = jnp.bfloat16
VMEM = pltpu.VMEM
SMEM = pltpu.SMEM
MIB = 1024 * 1024
IN_VMEM = pl.BlockSpec(memory_space=VMEM)
IN_SMEM = pl.BlockSpec(memory_space=SMEM)
IN_HBM = pl.BlockSpec(memory_space=pltpu.HBM)
ANYWHERE = pl.BlockSpec(memory_space=pl.ANY)


def params(mib):
    return pltpu.CompilerParams(vmem_limit_bytes=mib * MIB)


def cost(microseconds):
    return pl.CostEstimate(
        flops=int(microseconds * 0), bytes_accessed=int(microseconds * 0), transcendentals=0
    )


def normed(values, gains, scale):
    parts = []
    for first in range(0, values.shape[1], HD):
        head = values[:, first : first + HD]
        factor = lax.rsqrt(jnp.mean(head * head, axis=-1, keepdims=True) + EPS)
        parts.append(head * factor * gains[:, first : first + HD] * scale)
    return jnp.concatenate(parts, axis=1)


def project_kernel(steps, tokens, w_qkv, gains, near_mask, far_pattern, kv_out, queries_out, *scratch):
    token_buf, w_buf, gain_buf, near_buf, far_buf, total, kv, queries, sems, small_sems = scratch
    rows, width = tokens.shape
    count, _, cols = w_qkv.shape
    deep = width // steps
    copies = []
    for s in range(steps):
        span = pl.ds(s * deep, deep)
        group = [pltpu.make_async_copy(tokens.at[:, span], token_buf.at[:, span], sems.at[0, s])]
        for j in range(count):
            group.append(
                pltpu.make_async_copy(
                    w_qkv.at[j, span], w_buf.at[span, pl.ds(j * cols, cols)], sems.at[1 + j, s]
                )
            )
        for copy in group:
            copy.start()
        copies.append(group)
    small = [
        pltpu.make_async_copy(source, target, small_sems.at[i])
        for i, (source, target) in enumerate(
            ((gains, gain_buf), (near_mask, near_buf), (far_pattern, far_buf))
        )
    ]
    for copy in small:
        copy.start()
    for s in range(steps):
        for copy in copies[s]:
            copy.wait()
        span = slice(s * deep, (s + 1) * deep)
        part = jnp.dot(token_buf[:, span], w_buf[span, :], preferred_element_type=F32)
        if s == 0:
            total[...] = part
        elif s < steps - 1:
            total[...] += part
    part = total[...] + part
    for copy in small:
        copy.wait()
    query, key, value = (part[:, j * cols : (j + 1) * cols] for j in range(count))
    stores = [
        pltpu.make_async_copy(kv.at[pl.ds(0, rows)], kv_out.at[pl.ds(0, rows)], small_sems.at[3]),
        pltpu.make_async_copy(kv.at[pl.ds(rows, rows)], kv_out.at[pl.ds(rows, rows)], small_sems.at[4]),
        pltpu.make_async_copy(queries, queries_out, small_sems.at[5]),
    ]
    kv[rows:, :] = value.astype(BF16)
    stores[1].start()
    kv[:rows, :] = normed(key, gain_buf[1:2, :], 1.0).astype(BF16)
    stores[0].start()
    queries[:rows, :] = normed(query, gain_buf[0:1, :], HD ** (-0.5)).astype(BF16)
    n_blocks, n_near = near_mask.shape
    queries[rows:, :] = jnp.zeros((PAD, cols), BF16)
    queries[rows : rows + n_blocks, :n_near] = near_buf[...].astype(F32).astype(BF16)
    queries[rows : rows + n_blocks, HD : HD + far_pattern.shape[1]] = (
        far_buf[...].astype(F32).astype(BF16)
    )
    stores[2].start()
    for store in stores:
        store.wait()


def project(tokens, w_qkv, gains, near_mask, far_pattern):
    rows, width = tokens.shape
    count, _, cols = w_qkv.shape
    steps = 4
    return pl.pallas_call(
        functools.partial(project_kernel, steps),
        in_specs=[ANYWHERE] * 5,
        out_specs=[ANYWHERE] * 2,
        out_shape=[
            jax.ShapeDtypeStruct((2 * rows, cols), BF16),
            jax.ShapeDtypeStruct((rows + PAD, cols), BF16),
        ],
        scratch_shapes=[
            VMEM((rows, width), BF16),
            VMEM((width, count * cols), BF16),
            VMEM(gains.shape, F32),
            VMEM(near_mask.shape, jnp.int32),
            VMEM(far_pattern.shape, jnp.int32),
            VMEM((rows, count * cols), F32),
            VMEM((2 * rows, cols), BF16),
            VMEM((rows + PAD, cols), BF16),
            pltpu.SemaphoreType.DMA((1 + count, steps)),
            pltpu.SemaphoreType.DMA((6,)),
        ],
        compiler_params=params(56),
        cost_estimate=cost(5.0),
        name="project",
    )(tokens, w_qkv, gains, near_mask, far_pattern)


def split_sum(values):
    high = values.astype(BF16).astype(F32)
    mid = (values - high).astype(BF16).astype(F32)
    return high, mid, values - high - mid


def columns_kernel(n_head, w_out, _, payload, sems):
    cols = payload.shape[2]
    place = lax.axis_index("head")
    copies = []
    for k in range(1, n_head):
        first = pl.multiple_of(lax.rem(place + k, n_head) * cols, HD)
        copies.append(
            pltpu.make_async_copy(w_out.at[:, pl.ds(first, cols)], payload.at[k - 1], sems.at[k - 1])
        )
    for copy in copies:
        copy.start()
    for copy in copies:
        copy.wait()


def columns_of(w_out, n_head, before):
    rows, width = w_out.shape
    return pl.pallas_call(
        functools.partial(columns_kernel, n_head),
        in_specs=[ANYWHERE, IN_VMEM],
        out_specs=IN_VMEM,
        out_shape=jax.ShapeDtypeStruct((n_head - 1, rows, width // n_head), BF16),
        scratch_shapes=[pltpu.SemaphoreType.DMA((n_head - 1,))],
        compiler_params=params(16),
        cost_estimate=cost(1.0),
        name="columns",
    )(w_out, before)


def sums_kernel(w_out, _, sums):
    rows, width = w_out.shape
    total = lax.dot_general(
        jnp.ones((8, width), BF16), w_out[...], (((1,), (1,)), ((), ())), preferred_element_type=F32
    )
    high, mid, low = split_sum(total)
    row = lax.broadcasted_iota(jnp.int32, (8, rows), 0)
    packed = jnp.where(row == 0, high, jnp.where(row == 1, mid, jnp.where(row == 2, low, 0.0)))
    sums[...] = jnp.concatenate([packed, jnp.zeros((PAD - 8, rows), F32)], axis=0).astype(BF16)


def row_sums(w_out, before):
    return pl.pallas_call(
        sums_kernel,
        in_specs=[IN_VMEM] * 2,
        out_specs=IN_VMEM,
        out_shape=jax.ShapeDtypeStruct((PAD, w_out.shape[0]), BF16),
        compiler_params=params(16),
        cost_estimate=cost(0.8),
        name="row_sums",
    )(w_out, before)


def bias_kernel(side, n_slabs, n_blocks, ids, window, queries, _, out):
    rows = n_blocks * BLK
    shifted = lax.broadcasted_iota(jnp.int32, (BLK, BLK), 0) - lax.broadcasted_iota(
        jnp.int32, (BLK, BLK), 1
    )
    gaps = {
        by: jnp.abs(shifted + by * BLK).astype(F32) for by in range(1 - n_blocks, n_blocks)
    }
    lane = lax.broadcasted_iota(jnp.int32, (PAD, queries.shape[1]), 1)
    masks = queries[rows : rows + PAD, :].astype(F32)
    query_slab = ids[side]
    for c in range(n_slabs):
        key_slab = ids[4 + c]
        distance = jnp.abs(key_slab - query_slab)
        before = jnp.where(key_slab < query_slab, 0, 1)
        first = jnp.where(distance == 1, before * n_blocks, HD + key_slab * n_blocks)
        whole = jnp.where(distance == 0, 1.0, 0.0)
        reach = window[distance].astype(F32)
        for j in range(n_blocks):
            picked = jnp.sum(jnp.where(lane == first + j, masks, 0.0), axis=1, keepdims=True)
            limit = jnp.where(jnp.maximum(picked, whole) > 0.5, reach, 0.0)
            for i in range(n_blocks):
                here = jnp.broadcast_to(limit[i : i + 1, :], (BLK, BLK))
                out[c, i * BLK : (i + 1) * BLK, j * BLK : (j + 1) * BLK] = jnp.where(
                    gaps[i - j] < here, 0.0, BARRED
                )


def table_kernel(sides, n_slabs, n_blocks, ids, window, _, *tables):
    for side, table in zip(sides, tables):
        lanes, cols = table.shape
        lane = lax.broadcasted_iota(jnp.int32, (lanes, cols), 0)
        col = lax.broadcasted_iota(jnp.int32, (lanes, cols), 1)
        value = jnp.zeros((lanes, cols), F32)
        query_slab = ids[side]
        for c in range(n_slabs):
            key_slab = ids[4 + c]
            distance = jnp.abs(key_slab - query_slab)
            before = jnp.where(key_slab < query_slab, 0, 1)
            first = jnp.where(distance == 1, before * n_blocks, HD + key_slab * n_blocks)
            reach = window[distance].astype(F32)
            here = (lane - first == col - c * n_blocks) & (col // n_blocks == c)
            value = jnp.where(here, reach, value)
        table[...] = value.astype(BF16)


def tables(sides, ids, window, lanes, n_blocks, before):
    n_slabs = ids.shape[0] - 4
    return pl.pallas_call(
        functools.partial(table_kernel, sides, n_slabs, n_blocks),
        in_specs=[IN_SMEM] * 2 + [IN_VMEM],
        out_specs=[IN_VMEM] * len(sides),
        out_shape=[jax.ShapeDtypeStruct((lanes, HD), BF16) for _ in sides],
        compiler_params=params(16),
        cost_estimate=cost(0.5),
        name="tables",
    )(ids, window, before)


def late_bias_kernel(n_slabs, n_blocks, table, queries, _, out):
    rows = n_blocks * BLK
    limits = jnp.dot(queries[rows : rows + PAD, :], table[...], preferred_element_type=F32)
    shifted = lax.broadcasted_iota(jnp.int32, (BLK, BLK), 0) - lax.broadcasted_iota(
        jnp.int32, (BLK, BLK), 1
    )
    gaps = {
        by: jnp.abs(shifted + by * BLK).astype(F32) for by in range(1 - n_blocks, n_blocks)
    }
    for c in range(n_slabs):
        for i in range(n_blocks):
            for j in range(n_blocks):
                at = c * n_blocks + j
                here = jnp.broadcast_to(limits[i : i + 1, at : at + 1], (BLK, BLK))
                out[c, i * BLK : (i + 1) * BLK, j * BLK : (j + 1) * BLK] = jnp.where(
                    gaps[i - j] < here, 0.0, BARRED
                )


def biases(side, ids, window, queries, n_blocks, before):
    n_slabs = ids.shape[0] - 4
    rows = n_blocks * BLK
    return pl.pallas_call(
        functools.partial(bias_kernel, side, n_slabs, n_blocks),
        in_specs=[IN_SMEM] * 2 + [IN_VMEM] * 2,
        out_specs=IN_VMEM,
        out_shape=jax.ShapeDtypeStruct((n_slabs, rows, rows), F32),
        compiler_params=params(16),
        cost_estimate=cost(0.5),
        name="biases",
    )(ids, window, queries, before)


def attend_body(slabs, packed, heads, bias, queries, chunks, before, out):
    rows = bias.shape[1]
    ones = jnp.ones((rows, HD), BF16)
    if packed:
        out[rows:, :] = jnp.zeros((PAD, out.shape[1]), BF16)
    for h in range(*heads):
        span = slice(h * HD, (h + 1) * HD)
        keys = jnp.concatenate([key[:, span] for key, _ in chunks], axis=0)
        scores = lax.dot_general(
            queries[:rows, span], keys, (((1,), (1,)), ((), ())), preferred_element_type=F32
        )
        weights = [
            jnp.exp(scores[:, n * rows : (n + 1) * rows] + bias[slab]).astype(BF16)
            for n, slab in enumerate(slabs)
        ]
        values = jnp.concatenate(
            [jnp.concatenate([value[:, span], ones], axis=1) for _, value in chunks], axis=0
        )
        sums = jnp.dot(jnp.concatenate(weights, axis=1), values, preferred_element_type=F32)
        if before is not None:
            sums = sums + before[h]
        if not packed:
            out[h] = sums
            continue
        span = slice((h - heads[0]) * HD, (h - heads[0] + 1) * HD)
        out[:rows, span] = sums[:, :HD].astype(BF16)
        for b in range(rows // HD):
            pack_denominator(out, rows, b, span, sums[b * HD : (b + 1) * HD, HD:])


def taken_chunks(lone, rows, refs):
    chunks = []
    for apart in lone:
        if apart:
            keys, values = refs.pop(0), refs.pop(0)
            chunks.append((keys.at[:rows], values.at[values.shape[0] - rows :]))
        else:
            both = refs.pop(0)
            chunks.append((both.at[:rows], both.at[rows:]))
    return chunks


def other_kernel(slabs, lone, heads, n_blocks, table, queries, _, *refs):
    refs = list(refs)
    rows = n_blocks * BLK
    chunks = taken_chunks(lone, rows, refs)
    out, bias = refs
    late_bias_kernel(bias.shape[0], n_blocks, table, queries, None, bias)
    attend_body(slabs, False, heads, bias, queries, chunks, None, out)


def attend_other(table, queries, before, parts, n_slabs, n_blocks, heads, name):
    rows = n_blocks * BLK
    operands = [table, queries, before] + [array for chunk, _ in parts for array in chunk]
    return pl.pallas_call(
        functools.partial(
            other_kernel, [s for _, s in parts], [len(c) > 1 for c, _ in parts], heads, n_blocks
        ),
        in_specs=[IN_VMEM] * len(operands),
        out_specs=[IN_VMEM] * 2,
        out_shape=[
            jax.ShapeDtypeStruct((heads[1] - heads[0], rows, 2 * HD), F32),
            jax.ShapeDtypeStruct((n_slabs, rows, rows), F32),
        ],
        compiler_params=params(24),
        cost_estimate=cost(1.0),
        name=name,
    )(*operands)


def attend_kernel(slabs, lone, has_totals, heads, bias, queries, _, *refs):
    refs = list(refs)
    chunks = taken_chunks(lone, bias.shape[1], refs)
    before, out = (refs[0], refs[1]) if has_totals else (None, refs[0])
    attend_body(slabs, False, heads, bias, queries, chunks, before, out)


def pair_kernel(slabs, lone, heads, first_bias, first, second_bias, second, *refs):
    refs = list(refs)
    rows = first_bias.shape[1]
    chunks = taken_chunks(lone, rows, refs)
    first_totals, second_totals, out = refs
    held = rows + PAD
    attend_body(slabs, True, heads, first_bias, first, chunks, first_totals, out.at[:held])
    attend_body(slabs, True, heads, second_bias, second, chunks, second_totals, out.at[held:])


def attend_pair(first, second, parts, heads, name):
    rows = first[0].shape[1]
    operands = [first[0], first[1], second[0], second[1]]
    operands += [array for chunk, _ in parts for array in chunk] + [first[2], second[2]]
    return pl.pallas_call(
        functools.partial(
            pair_kernel, [slab for _, slab in parts], [len(c) > 1 for c, _ in parts], heads
        ),
        in_specs=[IN_VMEM] * len(operands),
        out_specs=IN_VMEM,
        out_shape=jax.ShapeDtypeStruct((2 * (rows + PAD), (heads[1] - heads[0]) * HD), BF16),
        compiler_params=params(24),
        cost_estimate=cost(0.6),
        name=name,
    )(*operands)


def attend(bias, queries, before, parts, totals, heads, name):
    rows = bias.shape[1]
    operands = [bias, queries, before] + [array for chunk, _ in parts for array in chunk]
    if totals is not None:
        operands.append(totals)
    count = heads[1] - heads[0]
    shape = jax.ShapeDtypeStruct((count, rows, 2 * HD), F32)
    slabs = [slab for _, slab in parts]
    return pl.pallas_call(
        functools.partial(
            attend_kernel, slabs, [len(c) > 1 for c, _ in parts], totals is not None, heads
        ),
        in_specs=[IN_VMEM] * len(operands),
        out_specs=IN_VMEM,
        out_shape=shape,
        compiler_params=params(24),
        cost_estimate=cost(0.08 * len(parts) * count + 0.15),
        name=name,
    )(*operands)


def packed_sums(packed, first, rows, block, span):
    here = slice(first + block * HD, first + (block + 1) * HD)
    pair = packed[first + rows : first + rows + PAD, span].astype(F32)
    row = pair[2 * block : 2 * block + 1, :] + pair[2 * block + 1 : 2 * block + 2, :]
    return packed[here, span].astype(F32), jnp.broadcast_to(row, (HD, HD)).T


def pack_denominator(out, rows, block, span, denominator):
    row = denominator.T[0:1, :]
    high = row.astype(BF16)
    out[rows + 2 * block : rows + 2 * block + 1, span] = high
    out[rows + 2 * block + 1 : rows + 2 * block + 2, span] = (row - high.astype(F32)).astype(BF16)


def join_kernel(last, firsts, kept, *refs):
    got, out = refs[:-2], refs[-1]
    heads, rows, _ = kept.shape
    if not last:
        out[rows:, :] = jnp.zeros((PAD, out.shape[1]), BF16)
    for h in range(heads):
        span = slice(h * HD, (h + 1) * HD)
        for b in range(rows // HD):
            here = slice(b * HD, (b + 1) * HD)
            num, den = kept[h, here, :HD], kept[h, here, HD:]
            for first, packed in zip(firsts, got):
                more_num, more_den = packed_sums(packed, first, rows, b, span)
                num, den = num + more_num, den + more_den
            if last:
                out[here, span] = (num / den).astype(BF16)
            else:
                out[here, span] = num.astype(BF16)
                pack_denominator(out, rows, b, span, den)


def join(kept, got, last, before):
    heads, rows, _ = kept.shape
    return pl.pallas_call(
        functools.partial(join_kernel, last, [first for _, first in got]),
        in_specs=[IN_VMEM] * (2 + len(got)),
        out_specs=IN_VMEM,
        out_shape=jax.ShapeDtypeStruct((rows + (0 if last else PAD), heads * HD), BF16),
        compiler_params=params(16),
        cost_estimate=cost(0.15),
        name="finish" if last else "join",
    )(kept, *[array for array, _ in got], before)


def gate_kernel(array, _, out):
    out[...] = array[...]


def gate_all_kernel(*refs):
    n = len(refs) // 2
    for array, out in zip(refs[:n], refs[n + 1 :]):
        out[...] = array[...]


def gate_all(arrays, before):
    n = len(arrays)
    return pl.pallas_call(
        gate_all_kernel,
        in_specs=[IN_VMEM] * (n + 1),
        out_specs=[IN_VMEM] * n,
        out_shape=[jax.ShapeDtypeStruct(array.shape, array.dtype) for array in arrays],
        input_output_aliases={i: i for i in range(n)},
        compiler_params=params(16),
        cost_estimate=cost(0.1),
        name="gate_all",
    )(*arrays, before)


def copy_kernel(array, _, out):
    out[...] = array[...]


def copied(array, before):
    return pl.pallas_call(
        copy_kernel,
        in_specs=[IN_VMEM] * 2,
        out_specs=IN_VMEM,
        out_shape=jax.ShapeDtypeStruct(array.shape, array.dtype),
        compiler_params=params(16),
        cost_estimate=cost(0.1),
        name="copied",
    )(array, before)


def gate(array, before):
    return pl.pallas_call(
        gate_kernel,
        in_specs=[IN_VMEM] * 2,
        out_specs=IN_VMEM,
        out_shape=jax.ShapeDtypeStruct(array.shape, array.dtype),
        input_output_aliases={0: 0},
        compiler_params=params(16),
        cost_estimate=cost(0.1),
        name="gate",
    )(array, before)


def row_dot(summed, values):
    dots = lax.dot_general(
        summed, values, (((1,), (1,)), ((), ())), preferred_element_type=F32
    )
    return dots[0:1, :] + (dots[1:2, :] + dots[2:3, :])


def early_kernel(n_head, place, own, w_out, sums, received, partial, parts, owners, held):
    cols = partial.shape[1]
    first = pl.multiple_of(place[0] * cols, HD)
    partial[...] = jnp.dot(own[...], w_out[:, pl.ds(first, cols)], preferred_element_type=F32)
    held[...] = received[...]
    parts[...] = jnp.zeros(parts.shape, F32)
    parts[pl.ds(place[0], 1), :] = row_dot(sums[...], own[...])
    row = lax.broadcasted_iota(jnp.int32, parts.shape, 0)
    for k in range(1, n_head):
        owner = lax.rem(place[0] - k + n_head, n_head)
        owners[k - 1] = jnp.where(row == owner, 1.0, 0.0)


def project_early(place, own, w_out, sums, received, n_head):
    rows = own.shape[0]
    cols = w_out.shape[1] // n_head
    places = -(-n_head // 8) * 8
    return pl.pallas_call(
        functools.partial(early_kernel, n_head),
        in_specs=[IN_SMEM] + [IN_VMEM] * 4,
        out_specs=[IN_VMEM] * 4,
        out_shape=[
            jax.ShapeDtypeStruct((rows, cols), F32),
            jax.ShapeDtypeStruct((places, rows), F32),
            jax.ShapeDtypeStruct((n_head - 1, places, rows), F32),
            jax.ShapeDtypeStruct(received.shape, BF16),
        ],
        compiler_params=params(24),
        cost_estimate=cost(1.4),
        name="project_early",
    )(place, own, w_out, sums, received)


def last_kernel(n_head, *refs):
    late, refs = refs[: n_head - 1], refs[n_head - 1 :]
    received, sums, partial, parts, owners, layer_out, checksum, staged, summed, sems = refs
    rows, cols = partial.shape
    tiles = sems.shape[0] - 1
    tile = cols // tiles
    stores = []
    for t in range(tiles):
        here = slice(t * tile, (t + 1) * tile)
        total = partial[:, here]
        for k in range(1, n_head):
            total = total + jnp.dot(
                late[k - 1][...], received[k - 1, :, here], preferred_element_type=F32
            )
        staged[:, here] = total.astype(BF16)
        there = pl.ds(t * tile, tile)
        stores.append(
            pltpu.make_async_copy(staged.at[:, there], layer_out.at[:, there], sems.at[t])
        )
        stores[-1].start()
        if t > 0:
            continue
        every = parts[...]
        for k in range(1, n_head):
            dot = row_dot(sums[(k - 1) * PAD : k * PAD, :], late[k - 1][...])
            every = every + owners[k - 1] * dot
        sum_all = every[0:1, :]
        for k in range(1, n_head):
            sum_all = sum_all + every[k : k + 1, :]
        summed[...] = sum_all * D ** (-0.5)
        stores.append(pltpu.make_async_copy(summed, checksum, sems.at[tiles]))
        stores[-1].start()
    for store in stores:
        store.wait()


def project_last(late, received, sums, partial, parts, owners):
    n_head = len(late) + 1
    rows, cols = partial.shape
    tiles = next(t for t in (3, 2, 1) if cols % (t * HD) == 0)
    operands = [*late, received, sums, partial, parts, owners]
    layer_out, checksum = pl.pallas_call(
        functools.partial(last_kernel, n_head),
        in_specs=[IN_VMEM] * len(operands),
        out_specs=[ANYWHERE] * 2,
        out_shape=[
            jax.ShapeDtypeStruct((rows, cols), BF16),
            jax.ShapeDtypeStruct((1, rows), F32),
        ],
        scratch_shapes=[
            VMEM((rows, cols), BF16),
            VMEM((1, rows), F32),
            pltpu.SemaphoreType.DMA((tiles + 1,)),
        ],
        compiler_params=params(24),
        name="project_last",
    )(*operands)
    return layer_out, checksum.reshape(rows)


def per_device(tokens, w_qkv, norm_gains, w_out, near_mask, far_pattern, window):
    rows = tokens.shape[0]
    heads = w_qkv.shape[2] // HD
    n_blocks = rows // BLK
    frame = lax.axis_index("frame").astype(jnp.int32)
    place = lax.axis_index("head").astype(jnp.int32).reshape(1)
    n_frame = lax.axis_size("frame")
    n_head = lax.axis_size("head")
    half = n_frame // 2
    every = (0, heads)

    def swapped(array, by):
        return lax.ppermute(array, "frame", [(i, i ^ by) for i in range(n_frame)])

    def from_head(array, k):
        return lax.ppermute(array, "head", [(i, (i + k) % n_head) for i in range(n_head)])

    def from_heads(arrays):
        got = [from_head(array, k) for k, array in enumerate(arrays, 1)]
        return got[0] if len(got) == 1 else jnp.concatenate(got)

    spans = []
    by = half // 2
    while by > 1:
        spans.append(by)
        by //= 2
    far = sorted((o for o in range(2, half, 2) if o not in spans), key=lambda o: bin(o).count("1"))
    slabs = [0] + spans + far
    n_near = 1 + len(spans)

    kv, queries = project(tokens, w_qkv, norm_gains, near_mask, far_pattern)
    near = {by: swapped(kv, by) for by in spans}
    sib_queries = swapped(queries, 1)
    ids = jnp.stack([frame ^ o for o in [0, 1, half, half ^ 1] + slabs])

    def bias_of(side, array, before):
        return biases(side, ids, window, array, n_blocks, before)

    mine = [((kv,), 0)]
    own_bias = bias_of(0, queries, queries)
    other_table, other_sib_table = tables(
        (2, 3), ids, window, queries.shape[1], n_blocks, own_bias
    )
    own = attend(own_bias, queries, other_sib_table, mine, None, every, "attend_first")
    other_queries = swapped(copied(queries, own), half)
    payload = columns_of(w_out, n_head, own)
    received = from_heads([payload[k - 1 : k] for k in range(1, n_head)])
    sib_bias = bias_of(1, sib_queries, own)
    sib = attend(sib_bias, sib_queries, sib_bias, mine, None, every, "sibling_first")

    near = dict(zip(spans, gate_all([near[by] for by in spans], sib)))
    keys = {by: near[by][: rows + 2 * PAD] for by in spans}
    values = {by: near[by][rows - 3 * PAD :] for by in spans}
    for o in far:
        bits = [by for by in spans if o & by]
        values[o] = swapped(values[o ^ bits[0]], bits[0])
        keys[o] = swapped(keys[o ^ bits[-1]], bits[-1])
    early = [((near[by],), i) for i, by in enumerate(spans, 1)]
    sib = attend(sib_bias, sib_queries, sib_bias, early, sib, every, "sibling_second")
    own = attend(own_bias, queries, sib, early, own, every, "attend_second")
    other_queries = gate(other_queries, own)
    other_sib = swapped(other_queries, 1)
    other, other_bias = attend_other(
        other_table, other_queries, own, mine + early, len(slabs), n_blocks, every, "other_first"
    )
    both, other_sib_bias = attend_other(
        other_sib_table, other_sib, other, mine + early, len(slabs), n_blocks, every, "other_sibling_first"
    )
    late = []
    for i, o in enumerate(far, n_near):
        late.append(((keys[o], values[o]), i))
    across = attend_pair(
        (other_sib_bias, other_sib, both), (sib_bias, sib_queries, sib), late, every, "attend_pair"
    )
    other = attend(other_bias, other_queries, across, late, other, every, "other_last")
    own = attend(own_bias, queries, other, late, own, every, "attend_last")
    from_core = swapped(across, 1)
    sent = join(other, [(from_core, 0)], False, own)
    got = swapped(sent, half)
    sums = row_sums(w_out, sent)
    done = join(own, [(from_core, rows + PAD), (got, 0)], True, sums)
    other_sums = from_heads([sums] * (n_head - 1))
    late = [from_head(done, k) for k in range(1, n_head)]
    partial, sum_parts, owners, received = project_early(
        place, done, w_out, sums, received, n_head
    )
    return project_last(late, received, other_sums, partial, sum_parts, owners)


def solution(mesh):
    in_specs = (
        P("frame", None),
        P(None, None, "head"),
        P(None, "head"),
        P("head", None),
        P("frame", None),
        P("frame", None),
        P(),
    )
    out_specs = (P("frame", "head"), P("frame"))
    return jax.shard_map(
        per_device, mesh=mesh, in_specs=in_specs, out_specs=out_specs, check_vma=False
    )
```
